128 devices in a mesh: fsdp: 8 (over y, core), context: 4 (over z), tensor: 4 (over x).
Axes of the slice: x: 4, y: 4, z: 4, core: 2. Of those that a mesh axis runs over, the one named last changes fastest.
Arguments:
- activations: bfloat16 [8, 1024, 2048], P('fsdp', 'context', 'tensor'), may hold values from -6 to 6
- segment_ids: int32 [8, 1024], P('fsdp'), may hold values from 0 to 3, as said below
- attn_gain: bfloat16 [2048], P(('fsdp', 'context')), may hold values from 0.5 to 1.5
- qkv_weight: bfloat16 [2048, 4096], P(('fsdp', 'context'), 'tensor'), may hold values from -0.125 to 0.125
- proj_weight: bfloat16 [2048, 2048], P('tensor', ('fsdp', 'context')), may hold values from -1 to 1
- ffn_gain: bfloat16 [2048], P(('fsdp', 'context')), may hold values from 0.5 to 1.5
- gate_weight: bfloat16 [2048, 8192], P(('fsdp', 'context'), 'tensor'), may hold values from -0.125 to 0.125
- up_weight: bfloat16 [2048, 8192], P(('fsdp', 'context'), 'tensor'), may hold values from -0.125 to 0.125
- down_weight: bfloat16 [8192, 2048], P('tensor', ('fsdp', 'context')), may hold values from -0.0625 to 0.0625
- cotangent: bfloat16 [8, 1024, 2048], P('fsdp', 'context', 'tensor'), may hold values from -6 to 6
- clip_limit: float32 [1], replicated, may hold values from 0.5 to 3
Outputs:
- output: bfloat16 [8, 1024, 2048], P('fsdp', 'context', 'tensor')
- input_grad: float32 [8, 1024, 2048], P('fsdp', 'context', 'tensor')
- query_key_value_gradient: float32 [2048, 4096], P(('fsdp', 'context'), 'tensor')
- projection_weight_gradient: float32 [2048, 2048], P('tensor', ('fsdp', 'context'))
- attngain_grad: float32 [2048], P(('fsdp', 'context'))
- gate_weight_gradient: float32 [2048, 8192], P(('fsdp', 'context'), 'tensor')
- up_weight_gradient: float32 [2048, 8192], P(('fsdp', 'context'), 'tensor')
- down_weight_gradient: float32 [8192, 2048], P('tensor', ('fsdp', 'context'))
- ffngain_grad: float32 [2048], P(('fsdp', 'context'))
- head_max: float32 [16], P('tensor')
- clipped_qkv: float32 [2048, 4096], P(('fsdp', 'context'), 'tensor')
The draws below stay inside these ranges and needn't reach their ends.
Inputs may be any that keep to these rules, and one draw needn't show every extreme that they name: `segment_ids`: each sequence holds exactly 4 documents, numbered 0 to 3 in order of place, each of 60 to 800 tokens; document 1 begins in the first quarter of its sequence and ends in the last quarter.
All inputs are finite; a program needn't handle non-finite values.
Results may differ from the reference program's by a relative error of at most 0.025.
Values may be sent and summed in bfloat16 or wider, within the bound.
No kernel may reach another device: no remote copies, remote signals or barrier semaphores. Data moves between devices by JAX's collectives and lax.ppermute only.
A program may use at most 128 MiB of HBM per device.

```python
import math
import jax
import jax.numpy as jnp
from jax import lax

D = 2048
HEADS = 16
KV_HEADS = 8
HEAD_DIM = 128
FF = 8192
LENGTH = 1024
SEQS = 8
QKV = 4096


def draw_segment_ids(key, part):
    key = jax.random.fold_in(key, 7)
    first_key, second_key, third_key = jax.random.split(key, 3)
    least = max(2, 60 * LENGTH // 1024)
    first_most = 200 * LENGTH // 1024
    span_most = 800 * LENGTH // 1024
    quarter = LENGTH // 4
    first_len = jax.random.randint(first_key, (SEQS,), least, first_most + 1)
    span_low = 3 * quarter + 1 - first_len
    span_high = jnp.minimum(span_most, LENGTH - 2 * least - first_len)
    span_len = jax.random.randint(second_key, (SEQS,), span_low, span_high + 1)
    remain = LENGTH - first_len - span_len
    third_len = jax.random.randint(third_key, (SEQS,), least, remain - least + 1)
    places = jnp.arange(LENGTH)[None, :]
    ends_one = first_len[:, None]
    ends_two = (first_len + span_len)[:, None]
    ends_three = (first_len + span_len + third_len)[:, None]
    ids = (places >= ends_one).astype(jnp.int32) + (places >= ends_two).astype(jnp.int32) + (places >= ends_three).astype(jnp.int32)
    return ids.astype(jnp.int32)


def block_scale(key, shape, pieces, smallest, high):
    gain, own = 1.0, jax.random.fold_in(key, 6)
    for position, shards_of in pieces:
        steps = jnp.exp(jax.random.uniform(jax.random.fold_in(own, position), (shards_of,), jnp.float32, smallest / len(pieces), high / len(pieces)))
        gain = gain * jnp.repeat(steps, shape[position] // shards_of).reshape([-1 if axis == position else 1 for axis in range(len(shape))])
    return gain


def scatter_about(own_key, dims, scale, limit, pieces=(), held_as=jnp.bfloat16):
    gain = block_scale(own_key, dims, pieces, -0.22, 0.18) if pieces else 1.0
    values = jax.random.normal(own_key, dims, jnp.float32) * scale * gain
    return jnp.minimum(jnp.maximum(values, -limit), limit).astype(held_as)


def setup_inputs(seed: int = 0) -> dict:
    arg_keys = jax.random.split(jax.random.key(seed), 12)
    activations = scatter_about(arg_keys[0], (SEQS, LENGTH, D), 1.0, 6.0, ((0, 8), (1, 4), (2, 4)))
    segment_ids = draw_segment_ids(jax.random.fold_in(arg_keys[11], 71), 0)
    attn_gain = jnp.clip(1.0 + 0.1 * jax.random.normal(arg_keys[2], (D,), jnp.float32), 0.5, 1.5).astype(jnp.bfloat16)
    qkv_weight = scatter_about(arg_keys[3], (D, QKV), D ** -0.5, 0.125, ((0, 32), (1, 4)))
    proj_weight = scatter_about(arg_keys[4], (HEADS * HEAD_DIM, D), (HEADS * HEAD_DIM // 64) ** -0.5, 1.0, ((0, 4), (1, 32)))
    ffn_gain = jnp.clip(1.0 + 0.1 * jax.random.normal(arg_keys[5], (D,), jnp.float32), 0.5, 1.5).astype(jnp.bfloat16)
    gate_weight = scatter_about(arg_keys[6], (D, FF), D ** -0.5, 0.125, ((0, 32), (1, 4)))
    up_weight = scatter_about(arg_keys[7], (D, FF), D ** -0.5, 0.125, ((0, 32), (1, 4)))
    down_weight = scatter_about(arg_keys[8], (FF, D), FF ** -0.5, 0.0625, ((0, 4), (1, 32)))
    cotangent = scatter_about(arg_keys[9], (SEQS, LENGTH, D), 1.0, 6.0, ((0, 8), (1, 4), (2, 4)))
    clip_limit = jnp.clip(jnp.exp(jax.random.uniform(arg_keys[10], (1,), jnp.float32, math.log(0.5), math.log(3.0))), 0.5, 3.0)
    return {"activations": activations, "segment_ids": segment_ids, "attn_gain": attn_gain, "qkv_weight": qkv_weight, "proj_weight": proj_weight, "ffn_gain": ffn_gain, "gate_weight": gate_weight, "up_weight": up_weight, "down_weight": down_weight, "cotangent": cotangent, "clip_limit": clip_limit}


EPS = 1e-05
THETA = 1000000.0
HIGH = lax.Precision.HIGHEST

@jax.custom_vjp
def low(v):
    return lax.optimization_barrier(v.astype(jnp.bfloat16)).astype(jnp.float32)

@jax.custom_vjp
def low_back(v):
    return v

def low_keep(v):
    return (low(v), None)

def low_pass(kept, grad):
    return (grad,)

def back_keep(v):
    return (v, None)

def back_low(kept, grad):
    return (low(grad),)
low.defvjp(low_keep, low_pass)
low_back.defvjp(back_keep, back_low)

def matmul(left, right):
    return jnp.einsum('...d,dc->...c', left, right, precision=HIGH)

def inverse_rms(values):
    return lax.rsqrt(lax.optimization_barrier(jnp.mean(values * values, axis=-1, keepdims=True)) + EPS)

def rope_tables(start, count, width):
    half = width // 2
    freqs = 1.0 / THETA ** (jnp.arange(half, dtype=jnp.float32) * 2.0 / width)
    places = (start + jnp.arange(count)).astype(jnp.float32)
    angles = places[:, None] * freqs[None, :]
    angles = jnp.concatenate([angles, angles], axis=-1)
    return (jnp.cos(angles), jnp.sin(angles))

def rotate_half(values):
    half = values.shape[-1] // 2
    return jnp.concatenate([-values[..., half:], values[..., :half]], axis=-1)

def apply_rope(values, cosine, sine):
    return values * cosine + rotate_half(values) * sine

def attend(operands):
    queries, keys, values, doc_ids = operands
    length = doc_ids.shape[0]
    places = jnp.arange(length)
    allowed = (doc_ids[:, None] == doc_ids[None, :]) & (places[None, :] <= places[:, None])
    raw = low_back(jnp.einsum('qgnh,kgh->gnqk', queries, keys, precision=HIGH))
    scores = raw * HEAD_DIM ** (-0.5)
    probs = jax.nn.softmax(jnp.where(allowed, scores, -1e+30), axis=-1)
    peak = lax.optimization_barrier(jnp.max(jnp.where(allowed, scores, -jnp.inf), axis=(2, 3)))
    attended = jnp.einsum('gnqk,kgh->qgnh', low(probs), values, precision=HIGH)
    return (attended, peak)

def forward(rows, gain_one, qkv_w, proj_w, gain_two, gate_w, up_w, down_w, doc_ids):
    seqs, length, width = rows.shape
    first_normalized = low(rows * inverse_rms(rows) * gain_one)
    projected_output = low_back(matmul(first_normalized, qkv_w))
    packed = projected_output.reshape(seqs, length, KV_HEADS, 4, HEAD_DIM)
    cosine, sine = rope_tables(0, length, HEAD_DIM)
    queries = low(apply_rope(packed[:, :, :, 0:2, :], cosine[:, None, None, :], sine[:, None, None, :]))
    keys = low(apply_rope(packed[:, :, :, 2, :], cosine[:, None, :], sine[:, None, :]))
    values = low(packed[:, :, :, 3, :])
    attended, peaks = lax.map(jax.checkpoint(attend), (queries, keys, values, doc_ids))
    context_reduced = low(low_back(attended)).reshape(seqs, length, HEADS * HEAD_DIM)
    branch = low_back(matmul(context_reduced, proj_w))
    mid = rows + branch
    second_normalized = low(mid * inverse_rms(mid) * gain_two)
    gate_activation = low_back(matmul(second_normalized, gate_w))
    upper_activation = low_back(matmul(second_normalized, up_w))
    hidden_activation = low(jax.nn.silu(gate_activation) * upper_activation)
    return (mid + matmul(hidden_activation, down_w), lax.optimization_barrier(jnp.max(peaks, axis=0)).reshape(HEADS))

def reference(activations, segment_ids, attn_gain, qkv_weight, proj_weight, ffn_gain, gate_weight, up_weight, down_weight, cotangent, clip_limit):

    def wrapped(rows, gain_one, qkv_w, proj_w, gain_two, gate_w, up_w, down_w):
        return forward(rows, gain_one, qkv_w, proj_w, gain_two, gate_w, up_w, down_w, segment_ids)
    output, pullback, peaks = jax.vjp(wrapped, activations.astype(jnp.float32), attn_gain.astype(jnp.float32), qkv_weight.astype(jnp.float32), proj_weight.astype(jnp.float32), ffn_gain.astype(jnp.float32), gate_weight.astype(jnp.float32), up_weight.astype(jnp.float32), down_weight.astype(jnp.float32), has_aux=True)
    grads = pullback(cotangent.astype(jnp.float32))
    bound = clip_limit[0]
    factors = jnp.sqrt(bound / jnp.maximum(peaks, bound)).reshape(KV_HEADS, 2)
    column_scale = jnp.concatenate([factors, lax.optimization_barrier(jnp.min(factors, axis=1, keepdims=True)), jnp.ones((KV_HEADS, 1), jnp.float32)], axis=1)
    clipped = (qkv_weight.astype(jnp.float32).reshape(D, KV_HEADS, 4, HEAD_DIM) * column_scale[None, :, :, None]).reshape(D, QKV)
    return (output.astype(jnp.bfloat16), grads[0], grads[2], grads[3], grads[1], grads[5], grads[6], grads[7], grads[4], peaks, clipped)
```

```python
import jax
import jax.numpy as jnp
from jax import lax
from jax.experimental import pallas as pl
from jax.experimental.pallas import tpu as pltpu
from jax.sharding import Mesh
from jax.sharding import PartitionSpec as P

HEAD_DIM = 128
EPS = 1e-05
THETA = 1000000.0
BF = jnp.bfloat16
F32 = jnp.float32
MIB = 1024 * 1024

NN = (((1,), (0,)), ((), ()))
NT = (((1,), (1,)), ((), ()))
TN = (((0,), (0,)), ((), ()))


def dot(a, b, dims):
    return lax.dot_general(a, b, dims, preferred_element_type=F32)


def shape(dims, kind):
    return jax.ShapeDtypeStruct(dims, kind)


def vmem(mib):
    return pltpu.CompilerParams(vmem_limit_bytes=mib * MIB)


def cost(gflop, mib):
    return pl.CostEstimate(
        flops=int(gflop * 1e9), bytes_accessed=int(mib * MIB), transcendentals=0
    )


def shift(v, axis, k):
    n = lax.axis_size(axis)
    return lax.ppermute(v, axis, [(i, (i + k) % n) for i in range(n)])


def swap(v):
    return shift(v, "c", 1)


def column_half(w, which):
    half = w.shape[1] // 2
    return lax.dynamic_slice_in_dim(w, which * half, half, 1)


def by_core(core, own, other):
    return jnp.where(core == 0, jnp.stack([own, other]), jnp.stack([other, own]))


def place(pieces, at, dim):
    own = pieces[0]
    width = own.shape[dim]
    dims = own.shape[:dim] + (4 * width,) + own.shape[dim + 1 :]
    out = jnp.zeros(dims, own.dtype)
    for k, piece in pieces.items():
        out = lax.dynamic_update_slice_in_dim(out, piece, ((at + k) % 4) * width, dim)
    return out


def wave(*arrays):
    return lax.optimization_barrier(arrays)


def after(v, *others):
    return lax.optimization_barrier((v, *others))[0]


def direct(own, axis):
    return shift(own, axis, 1), shift(own, axis, -1), shift(own, axis, 2)


def halves_of(v, cut):
    half = v.shape[cut] // 2
    return lax.slice_in_dim(v, 0, half, axis=cut), lax.slice_in_dim(v, half, 2 * half, axis=cut)


def near_two(own, axis):
    return shift(own, axis, 1), shift(own, axis, -1)


def far_two(before, behind, axis, cut):
    return shift(halves_of(before, cut)[0], axis, 1), shift(halves_of(behind, cut)[1], axis, -1)


def placed(own, near, far, at, dim, cut):
    return place({0: own, -1: near[0], 1: near[1], 2: jnp.concatenate(far, axis=cut)}, at, dim)


def ring_block(v, at, k, dim):
    width = v.shape[dim] // 4
    return lax.dynamic_slice_in_dim(v, ((at + k) % 4) * width, width, dim)


def reduce_far(v, axis, at, dim, cut):
    low, high = halves_of(ring_block(v, at, 2, dim), cut)
    return shift(low, axis, 1), shift(high, axis, -1)


def reduce_near(v, far, axis, at, dim, cut):
    zeros = jnp.zeros_like(far[0])
    up = ring_block(v, at, 1, dim).astype(F32) + jnp.concatenate([far[0], zeros], axis=cut)
    down = ring_block(v, at, -1, dim).astype(F32) + jnp.concatenate([zeros, far[1]], axis=cut)
    return shift(up.astype(BF), axis, 1), shift(down.astype(BF), axis, -1)


def reduce_direct(v, axis, at, dim):
    return tuple(shift(ring_block(v, at, k, dim).astype(BF), axis, k) for k in (1, -1, 2))


def total(v, at, dim, parts):
    return sum((p.astype(F32) for p in parts), ring_block(v, at, 0, dim).astype(F32))


def along_x(v):
    return lax.ppermute(
        v, ("c", "x"), [(4 * c + x, 4 * c + (x + 1 - 2 * c) % 4) for c in (0, 1) for x in range(4)]
    )


def sum_far(keep, got):
    n = keep.shape[0] // 4
    return along_x((keep[2 * n : 3 * n].astype(F32) + got[2 * n : 3 * n].astype(F32)).astype(BF))


def sum_near(keep, got, far):
    n = keep.shape[0] // 4
    first = keep[:n].astype(F32) + got[:n].astype(F32) + far.astype(F32)
    second = keep[n : 2 * n].astype(F32) + got[n : 2 * n].astype(F32)
    return along_x(jnp.concatenate([first.astype(BF), second.astype(BF)], axis=0))


def sum_rest(near):
    return swap(near[near.shape[0] // 2 :])


def sum_all(keep, got, near, rest):
    n = keep.shape[0] // 4
    parts = (keep[3 * n :], got[3 * n :], near[:n], rest)
    return sum(p.astype(F32) for p in parts)


def swap_blocks(v, first, second):
    rows = v.shape[0]
    return v.reshape(rows, first, second, -1).swapaxes(1, 2).reshape(rows, -1)


def roll_half(v):
    return pltpu.roll(v, 64, 1)


def lanes(block):
    return pl.ds(pl.multiple_of(block * 512, 512), 512)


def assemble(at_ref, parts, out_ref):
    pair, near, other_near, far, other_far = parts
    count = far.shape[0]
    out_ref[:, lanes(at_ref[0])] = pair[...]
    out_ref[:, lanes(at_ref[1])] = near[...]
    out_ref[:count, lanes(at_ref[2])] = other_near[count:]
    out_ref[count:, lanes(at_ref[2])] = other_near[:count]
    out_ref[:count, lanes(at_ref[3])] = far[...]
    out_ref[count:, lanes(at_ref[3])] = other_far[...]


def part_specs(parts, column):
    return [pl.BlockSpec((p.shape[0], 512), lambda s, at: (0, column)) for p in parts]


def fixed(dims):
    return pl.BlockSpec(dims, lambda s, at: (0,) * len(dims))


def call(kernel, at, grid, args, in_specs, out_specs, out_shape, scratch, mib, name, work):
    return pl.pallas_call(
        kernel,
        grid_spec=pltpu.PrefetchScalarGridSpec(
            num_scalar_prefetch=1,
            grid=(grid,),
            in_specs=in_specs,
            out_specs=out_specs,
            scratch_shapes=scratch,
        ),
        out_shape=out_shape,
        compiler_params=vmem(mib),
        cost_estimate=cost(*work),
        name=name,
    )(at, *args)


def qkv_kernel(at_ref, *refs):
    parts, refs = refs[:5], refs[5:]
    gains_ref, w_ref, cos_ref, sin_ref, q_ref, kv_ref, nt_ref, row_ref, rows_ref, keep = refs
    step = pl.program_id(0)
    span = q_ref.shape[0]

    @pl.when(step == 0)
    def _():
        keep[...] = gains_ref[...].astype(F32).T[:8]
        row_ref[...] = keep[...]
        assemble(at_ref, parts, rows_ref)

    rows = rows_ref[pl.ds(pl.multiple_of(step * span, span), span)].astype(F32)
    scale = lax.rsqrt(jnp.mean(rows * rows, axis=-1, keepdims=True) + EPS)
    normed = (rows * scale * keep[0:1]).astype(BF)
    nt_ref[...] = normed.T
    projected = dot(normed, w_ref[...], NN)
    cosine, sine = cos_ref[...], sin_ref[...]
    out = []
    for i in range(3):
        v = projected[:, i * HEAD_DIM : (i + 1) * HEAD_DIM]
        out.append((v * cosine + roll_half(v) * sine).astype(BF))
    q_ref[...] = jnp.concatenate(out[:2], axis=1)
    kv_ref[0] = jnp.concatenate([out[2], projected[:, 3 * HEAD_DIM :].astype(BF)], axis=1)


def cot_kernel(at_ref, *refs):
    parts, (out_ref, flipped_ref) = refs[:5], refs[5:]
    assemble(at_ref, parts, out_ref)
    flipped_ref[...] = out_ref[...].T


def cot_call(at, parts):
    tokens, width = parts[0].shape[0], 4 * 512
    return call(
        cot_kernel,
        at,
        1,
        parts,
        part_specs(parts, 1),
        [fixed((tokens, width)), fixed((width, tokens))],
        [shape((tokens, width), BF), shape((width, tokens), BF)],
        [],
        20,
        "cotangent_rows",
        (0.5, 8),
    )


def qkv_call(at, parts, gains, w_qkv, cosine, sine):
    tokens, width = parts[0].shape[0], w_qkv.shape[0]
    span = tokens // 2
    cols = w_qkv.shape[1]
    return call(
        qkv_kernel,
        at,
        2,
        (*parts, gains, w_qkv, cosine, sine),
        part_specs(parts, 0)
        + [
            pl.BlockSpec((width, 128), lambda s, at: (0, 2)),
            fixed((width, cols)),
            fixed((span, HEAD_DIM)),
            fixed((span, HEAD_DIM)),
        ],
        [
            pl.BlockSpec((span, 2 * HEAD_DIM), lambda s, at: (s, 0)),
            pl.BlockSpec((1, span, 2 * HEAD_DIM), lambda s, at: (s, 0, 0)),
            pl.BlockSpec((width, span), lambda s, at: (0, s)),
            fixed((8, width)),
            fixed((tokens, width)),
        ],
        [
            shape((tokens, 2 * HEAD_DIM), BF),
            shape((2, span, 2 * HEAD_DIM), BF),
            shape((width, tokens), BF),
            shape((8, width), F32),
            shape((tokens, width), BF),
        ],
        [pltpu.VMEM((8, width), F32)],
        28,
        "norm_qkv_rope",
        (2.5, 10),
    )


def stacked(v):
    return jnp.concatenate([v[:, :HEAD_DIM], v[:, HEAD_DIM:]], axis=0)


def allowed_mask(low_ref, high_ref, length):
    low, high = low_ref[0], high_ref[...]
    places = lax.broadcasted_iota(jnp.int32, (length, low.shape[1]), 0)
    mask = (places >= low) & (places <= high)
    return jnp.concatenate([mask, mask], axis=1)


def attend_kernel(q_ref, kv_ref, low_ref, high_ref, out_ref, lse_ref, peak_ref):
    length = kv_ref.shape[1]
    span = q_ref.shape[0]
    queries = stacked(q_ref[...])
    keys, values = kv_ref[0, :, :HEAD_DIM], kv_ref[0, :, HEAD_DIM:]
    raw = dot(keys, queries, NT)
    scores = jnp.where(allowed_mask(low_ref, high_ref, length), raw * HEAD_DIM**-0.5, -1e30)
    largest = jnp.max(scores, axis=0, keepdims=True)
    weights = jnp.exp(scores - largest)
    total = jnp.sum(weights, axis=0, keepdims=True)
    probs = (weights * (1.0 / total)).astype(BF)
    attended = dot(values, probs, TN).T.astype(BF)
    out_ref[...] = jnp.concatenate([attended[:span], attended[span:]], axis=1)
    lse_ref[0] = largest + jnp.log(total)
    tops = [jnp.max(largest[:, h * span : (h + 1) * span], axis=1, keepdims=True) for h in (0, 1)]
    peak_ref[0] = jnp.concatenate([jnp.broadcast_to(t, (4, 128)) for t in tops], axis=0)


def attend_call(queries, kv, low, high):
    tokens = queries.shape[0]
    span, length, both = tokens // 2, kv.shape[1], 2 * HEAD_DIM
    return pl.pallas_call(
        attend_kernel,
        grid=(2,),
        in_specs=[
            pl.BlockSpec((span, both), lambda s: (s, 0)),
            pl.BlockSpec((1, length, both), lambda s: (s, 0, 0)),
            pl.BlockSpec((1, 1, span), lambda s: (s, 0, 0)),
            pl.BlockSpec((1, span), lambda s: (0, 0)),
        ],
        out_specs=[
            pl.BlockSpec((span, both), lambda s: (s, 0)),
            pl.BlockSpec((1, 1, 2 * span), lambda s: (s, 0, 0)),
            pl.BlockSpec((1, 8, 128), lambda s: (s, 0, 0)),
        ],
        out_shape=[
            shape((tokens, both), BF),
            shape((2, 1, 2 * span), F32),
            shape((2, 8, 128), F32),
        ],
        compiler_params=vmem(20),
        cost_estimate=cost(2.5, 4),
        name="attend",
    )(queries, kv, low, high)


def attend_back_kernel(
    q_ref, kv_ref, low_ref, high_ref, lse_ref, up_ref, cos_ref, sin_ref, dq_ref, dkv_ref
):
    length = kv_ref.shape[1]
    span = q_ref.shape[0]
    queries, upstream = stacked(q_ref[...]), stacked(up_ref[...])
    keys, values = kv_ref[0, :, :HEAD_DIM], kv_ref[0, :, HEAD_DIM:]
    raw = dot(keys, queries, NT)
    factor = HEAD_DIM**-0.5
    probs = jnp.where(
        allowed_mask(low_ref, high_ref, length), jnp.exp(raw * factor - lse_ref[0]), 0.0
    )
    dprobs = dot(values, upstream, NT)
    rowdot = jnp.sum(probs * dprobs, axis=0, keepdims=True)
    dscores = (probs * (dprobs - rowdot) * factor).astype(BF)
    dkey = dot(dscores, queries, NN)
    dvalue = dot(probs.astype(BF), upstream, NN)
    dkv_ref[0] = jnp.concatenate([dkey, dvalue], axis=1).astype(BF)
    dquery = dot(keys, dscores, TN).T
    cosine, sine = cos_ref[...], sin_ref[...]
    heads = []
    for h in (0, 1):
        d = dquery[h * span : (h + 1) * span]
        heads.append((d * cosine - roll_half(d) * sine).astype(BF))
    dq_ref[...] = jnp.concatenate(heads, axis=1)


def attend_back_call(queries, kv, low, high, lse, upstream, cosine, sine):
    tokens = queries.shape[0]
    span, length, both = tokens // 2, kv.shape[1], 2 * HEAD_DIM
    table = pl.BlockSpec((span, HEAD_DIM), lambda s: (0, 0))
    return pl.pallas_call(
        attend_back_kernel,
        grid=(2,),
        in_specs=[
            pl.BlockSpec((span, both), lambda s: (s, 0)),
            pl.BlockSpec((1, length, both), lambda s: (s, 0, 0)),
            pl.BlockSpec((1, 1, span), lambda s: (s, 0, 0)),
            pl.BlockSpec((1, span), lambda s: (0, 0)),
            pl.BlockSpec((1, 1, 2 * span), lambda s: (s, 0, 0)),
            pl.BlockSpec((span, both), lambda s: (s, 0)),
            table,
            table,
        ],
        out_specs=[
            pl.BlockSpec((span, both), lambda s: (s, 0)),
            pl.BlockSpec((1, length, both), lambda s: (s, 0, 0)),
        ],
        out_shape=[shape((tokens, both), BF), shape((2, length, both), BF)],
        compiler_params=vmem(28),
        cost_estimate=cost(4.5, 4),
        name="attend_back",
    )(queries, kv, low, high, lse, upstream, cosine, sine)


def ffn_kernel(at_ref, *refs):
    parts, refs = refs[:5], refs[5:]
    cot_ref, gain_ref, wg_ref, wu_ref, wd_ref, bg_ref, bu_ref = refs[:7]
    act_ref, normed_ref, keep_ref, give_ref, mid_ref, held, stat = refs[7:]
    step = pl.program_id(0)
    steps = pl.num_programs(0) - 4
    block = wg_ref.shape[1]

    @pl.when(step == 0)
    def _():
        assemble(at_ref, parts, mid_ref)

        @pl.loop(0, mid_ref.shape[0] // 128)
        def _(i):
            rows = pl.ds(pl.multiple_of(i * 128, 128), 128)
            mid = mid_ref[rows].astype(F32)
            scale = lax.rsqrt(jnp.mean(mid * mid, axis=-1, keepdims=True) + EPS)
            normed_ref[rows] = (mid * scale * gain_ref[1:2]).astype(BF)

    @pl.when(step < steps)
    def _():
        at = pl.ds(pl.multiple_of(step * block, block), block)
        normed = normed_ref[...]
        gate = dot(normed, wg_ref[...], NN)
        upper = dot(normed, wu_ref[...], NN)
        dhidden = dot(cot_ref[...], wd_ref[...], NN)
        sigmoid = 1.0 / (1.0 + jnp.exp(-gate))
        silu = gate * sigmoid
        slope = sigmoid * (1.0 + gate * (1.0 - sigmoid))
        act_ref[0, :, at] = (dhidden * upper * slope).astype(BF)
        act_ref[1, :, at] = (dhidden * silu).astype(BF)
        act_ref[2, :, at] = (silu * upper).astype(BF)

    @pl.when(step >= steps)
    def _():
        back = dot(act_ref[0], bg_ref[...], NT) + dot(act_ref[1], bu_ref[...], NT)
        back_step(back, step - steps, 1, at_ref, mid_ref, gain_ref, keep_ref, give_ref, held, stat)


def ffn_call(at, mid_parts, cot, gains, w):
    tokens, width = mid_parts[0].shape[0], w.shape[0]
    cols = w.shape[1] // 3
    block = 256
    steps = cols // block
    whole = fixed((tokens, width))

    def columns(i):
        return pl.BlockSpec((width, block), lambda j, at: (0, i * steps + jnp.minimum(j, steps - 1)))

    def rows(i):
        return pl.BlockSpec((width // 4, cols), lambda j, at: (jnp.maximum(j - steps, 0), i))

    moved = (2 * tokens, width // 4)
    return call(
        ffn_kernel,
        at,
        steps + 4,
        (*mid_parts, cot, gains, w, w, w, w, w),
        part_specs(mid_parts, 0)
        + [whole, fixed((8, width)), columns(0), columns(1), columns(2), rows(0), rows(1)],
        [fixed((3, tokens, cols)), whole, fixed(moved), fixed(moved)],
        [shape((3, tokens, cols), BF), shape((tokens, width), BF)] + [shape(moved, BF)] * 2,
        [
            pltpu.VMEM((tokens, width), BF),
            pltpu.VMEM((4, tokens, width // 4), F32),
            pltpu.VMEM((2, tokens, 128), F32),
        ],
        48,
        "ffn",
        (15, 28),
    )


def back_step(back, step, norm, at_ref, base_ref, gain_ref, keep_ref, give_ref, held, stat):
    held[step] = back
    if norm is not None:
        base = base_ref[:, lanes(step)].astype(F32)
        gain = gain_ref[norm : norm + 1, lanes(step)]
        inner = jnp.sum(base * (gain * back), axis=-1, keepdims=True)
        square = jnp.sum(base * base, axis=-1, keepdims=True)

        @pl.when(step == 0)
        def _():
            stat[0] = jnp.broadcast_to(inner, stat.shape[1:])
            stat[1] = jnp.broadcast_to(square, stat.shape[1:])

        @pl.when(step > 0)
        def _():
            stat[0] += jnp.broadcast_to(inner, stat.shape[1:])
            stat[1] += jnp.broadcast_to(square, stat.shape[1:])

    @pl.when(step == 3)
    def _():
        count = held.shape[1] // 2
        if norm is not None:
            width = 4 * held.shape[2]
            scale = lax.rsqrt(stat[1, :, 0:1] / width + EPS)
            factor = scale * scale * scale * stat[0, :, 0:1] / width

        def final(k):
            block = at_ref[k]
            v = held[block]
            if norm is not None:
                gain = gain_ref[norm : norm + 1, lanes(block)]
                v = scale * (gain * v) - base_ref[:, lanes(block)].astype(F32) * factor
            return v.astype(BF)

        keep_ref[: 2 * count] = final(2)
        v = final(1)
        give_ref[:count] = v[count:]
        give_ref[count : 2 * count] = v[:count]
        for k, row in ((3, 2), (0, 3)):
            v = final(k)
            keep_ref[row * count : (row + 1) * count] = v[:count]
            give_ref[row * count : (row + 1) * count] = v[count:]


def back_kernel(terms, norm, at_ref, *refs):
    a_refs, w_refs, refs = refs[:terms], refs[terms : 2 * terms], refs[2 * terms :]
    back = sum(dot(a[0], w[...], NT) for a, w in zip(a_refs, w_refs))
    if norm is None:
        refs = (None, None, *refs, None)
    back_step(back, pl.program_id(0), norm, at_ref, *refs)


def back_call(at, pairs, norm, extra, name):
    tokens, width = pairs[0][0].shape[1], pairs[0][2].shape[0]
    block = width // 4
    args, specs = [], []
    for a, i, _, _ in pairs:
        args.append(a)
        specs.append(pl.BlockSpec((1, tokens, a.shape[2]), lambda s, at, i=i: (i, 0, 0)))
    for a, _, w, j in pairs:
        args.append(w)
        specs.append(pl.BlockSpec((block, a.shape[2]), lambda s, at, j=j: (s, j)))
    scratch = [pltpu.VMEM((4, tokens, block), F32)]
    if norm is not None:
        specs += [fixed(v.shape) for v in extra]
        args += extra
        scratch.append(pltpu.VMEM((2, tokens, 128), F32))

    def kernel(*refs):
        back_kernel(len(pairs), norm, *refs)

    return call(
        kernel,
        at,
        4,
        args,
        specs,
        [fixed((2 * tokens, block))] * 2,
        [shape((2 * tokens, block), BF)] * 2,
        scratch,
        24,
        name,
        (sum(1.2e-9 * 2 * tokens * width * a.shape[2] for a, *_ in pairs) + 1, 8),
    )


def ffn_grad_kernel(normed_ref, cot_ref, act_ref, out_ref, flipped):
    step = pl.program_id(0)
    steps = pl.num_programs(0) // 3

    @pl.when(step == 0)
    def _():
        flipped[...] = normed_ref[...].T

    @pl.when(step < 2 * steps)
    def _():
        out_ref[...] = dot(flipped[...], act_ref[0], NN).astype(BF)

    @pl.when(step >= 2 * steps)
    def _():
        out_ref[...] = dot(cot_ref[...], act_ref[0], NN).astype(BF)


def ffn_grad_call(normed, cot_flipped, act):
    tokens, width = normed.shape
    block = 256
    steps = act.shape[2] // block
    return pl.pallas_call(
        ffn_grad_kernel,
        grid=(3 * steps,),
        in_specs=[
            pl.BlockSpec((tokens, width), lambda j: (0, 0)),
            pl.BlockSpec((width, tokens), lambda j: (0, 0)),
            pl.BlockSpec((1, tokens, block), lambda j: (j // steps, 0, j % steps)),
        ],
        out_specs=pl.BlockSpec((width, block), lambda j: (0, j)),
        out_shape=pltpu.HBM((width, 3 * steps * block), BF),
        scratch_shapes=[pltpu.VMEM((width, tokens), BF)],
        compiler_params=vmem(20),
        cost_estimate=cost(9, 20),
        name="ffn_grads",
    )(normed, cot_flipped, act)


def proj_kernel(at_ref, *refs):
    parts, (w_ref, att_ref, datt_ref, grad_ref, up) = refs[:5], refs[5:]
    assemble(at_ref, parts, up)
    datt_ref[...] = dot(up[...], w_ref[...], NN).astype(BF)
    grad_ref[...] = dot(att_ref[...], up[...], TN).T.astype(BF)


def proj_call(at, parts, w_proj, attended):
    tokens, cols = attended.shape
    width = w_proj.shape[0]
    return call(
        proj_kernel,
        at,
        1,
        (*parts, w_proj, attended),
        part_specs(parts, 0) + [fixed((width, cols)), fixed((tokens, cols))],
        [fixed((tokens, cols)), fixed((width, cols))],
        [shape((tokens, cols), BF), shape((width, cols), BF)],
        [pltpu.VMEM((tokens, width), BF)],
        20,
        "proj_back",
        (2.5, 6),
    )


def dkv_kernel(dq_ref, dkv_ref, cos_ref, sin_ref, nt_ref, d_ref, grad_ref):
    span = dkv_ref.shape[1]
    cosine, sine = cos_ref[...], sin_ref[...]
    d_ref[0, :, : 2 * HEAD_DIM] = dq_ref[...]
    for s in (0, 1):
        dk = dkv_ref[s, :, :HEAD_DIM]
        at = pl.ds(s * span, span)
        d_ref[0, at, 2 * HEAD_DIM : 3 * HEAD_DIM] = (dk * cosine - roll_half(dk) * sine).astype(BF)
        d_ref[0, at, 3 * HEAD_DIM :] = dkv_ref[s, :, HEAD_DIM:].astype(BF)
    grad_ref[...] = dot(nt_ref[...], d_ref[0, :, 2 * HEAD_DIM :], NN).astype(BF)


def dkv_call(dq, dkv, cosine, sine, nt):
    tokens, width = dq.shape[0], nt.shape[0]
    both = 2 * HEAD_DIM
    return pl.pallas_call(
        dkv_kernel,
        out_shape=[shape((1, tokens, 2 * both), BF), shape((width, both), BF)],
        compiler_params=vmem(16),
        cost_estimate=cost(0.8, 4),
        name="dkv",
    )(dq, dkv, cosine, sine, nt)


def local(
    activations,
    segment_ids,
    attn_gain,
    qkv_weight,
    proj_weight,
    ffn_gain,
    gate_weight,
    up_weight,
    down_weight,
    cotangent,
    clip_limit,
):
    core = lax.axis_index("c")
    at_x = lax.axis_index("x")
    at_y = lax.axis_index("y")
    at_z = lax.axis_index("z")
    _, span, width = activations.shape
    head_dim = HEAD_DIM
    rows_held = qkv_weight.shape[0]
    block = 2 * rows_held

    side = 1 - 2 * core
    at = jnp.stack([at_x, at_x - side, at_x + side, at_x + 2]).astype(jnp.int32) % 4

    gains = jnp.concatenate(
        [attn_gain[:, None], ffn_gain[:, None], jnp.zeros((rows_held, 126), BF)], axis=1
    )

    def halves(parts, extra):
        own = jnp.concatenate([column_half(w, core) for w in parts] + extra, axis=1)
        away = jnp.concatenate([column_half(w, 1 - core) for w in parts] + extra, axis=1)
        return own, away

    def both_rows(own, other):
        return by_core(core, own, other).reshape(block, -1)

    rows_mine = swap_blocks(activations[0], 2, 4)
    cot_mine = swap_blocks(cotangent[0], 2, 4)
    own_rows = jnp.concatenate([rows_mine, cot_mine], axis=1)
    attn_own, attn_away = halves((qkv_weight, proj_weight.T), [gains])
    ffn_own, ffn_away = halves((gate_weight, up_weight, down_weight.T), [])
    attn_other, rows_other, ids_other = wave(swap(attn_away), swap(own_rows), swap(segment_ids))
    attn_shard = both_rows(attn_own, attn_other)
    a0, b0 = attn_shard[None, :, : 4 * head_dim], attn_shard[None, :, 4 * head_dim :]
    pair = jnp.concatenate([own_rows, rows_other], axis=0)
    n = span

    *got, row_near, ffn_other = wave(
        *direct(a0, "y"), *direct(b0, "z"), along_x(pair), swap(ffn_away)
    )
    a1 = place(dict(zip((0, -1, 1, 2), (a0, *got[:3]))), at_y, 0)[:, None]
    b1 = place(dict(zip((0, -1, 1, 2), (b0, *got[3:]))), at_z, 0)[None]
    a_near_0, a_near_1, b_near_0, b_near_1, row_far, row_near_other = wave(
        *near_two(a1, "z"), *near_two(b1, "y"), along_x(row_near[:n]), swap(row_near)
    )
    ffn_shard = both_rows(ffn_own, after(ffn_other, a_near_0))
    w_ffn = lax.all_gather(ffn_shard, ("y", "z"), axis=0, tiled=True)
    a_far_0, a_far_1, b_far_0, b_far_1, row_far_other = wave(
        *far_two(a_near_0, a_near_1, "z", 2), *far_two(b_near_0, b_near_1, "y", 2), swap(row_far)
    )

    def in_rows(v):
        return v.reshape(16 * block, -1)

    w_qkv = in_rows(placed(a1, (a_near_0, a_near_1), (a_far_0, a_far_1), at_z, 1, 2))
    w_proj = in_rows(placed(b1, (b_near_0, b_near_1), (b_far_0, b_far_1), at_y, 0, 2))
    row_parts = (pair, row_near, row_near_other, row_far, row_far_other)

    half = head_dim // 2
    freqs = 1.0 / THETA ** (jnp.arange(half, dtype=F32) * 2.0 / head_dim)
    places = at_z * span + jnp.arange(span)
    angles = places.astype(F32)[:, None] * freqs[None, :]
    cosine = jnp.cos(jnp.concatenate([angles, angles], axis=1))
    sine = jnp.sin(angles)
    sine = jnp.concatenate([-sine, sine], axis=1)
    ids = jnp.concatenate([segment_ids, ids_other], axis=0)
    query_ids = lax.dynamic_slice_in_dim(ids, at_z * span, span, 1)
    low = jnp.sum(ids[:, :, None] < query_ids[:, None, :], axis=1, dtype=jnp.int32)[:, None, :]
    high = places.astype(jnp.int32)[None, :]

    queries, kv_mine, normed_one_t, gain_rows, rows = qkv_call(
        at, row_parts, w_proj, w_qkv, cosine, sine
    )
    kv_near = wave(*near_two(kv_mine, "z"))
    cot, cot_flipped = cot_call(at, (after(pair, kv_near[0]), *row_parts[1:]))
    *kv_far, cot, cot_flipped = wave(*far_two(*kv_near, "z", 1), cot, cot_flipped)
    kv = placed(kv_mine, kv_near, kv_far, at_z, 1, 1)
    attended, lse, peak = attend_call(queries, kv, low, high)
    peak = jnp.max(peak, axis=0)
    keep, give = back_call(at, [(attended[None], 0, w_proj, 0)], None, [], "branch")

    (got,) = wave(swap(give))
    far, other_peak = wave(sum_far(keep, got), shift(peak, "y", 1))
    peak = jnp.maximum(peak, other_peak)
    near, other_peak = wave(sum_near(keep, got, far), shift(peak, "y", 2))
    peak = jnp.maximum(peak, other_peak)
    (rest,) = wave(sum_rest(near))
    mid_mine = rows_mine.astype(F32) + sum_all(keep, got, near, rest)
    mid_low = mid_mine.astype(BF)
    (other,) = wave(swap(mid_low))
    pair = jnp.concatenate([mid_low, other], axis=0)
    near, other_peak = wave(along_x(pair), shift(peak, "z", 1))
    peak = jnp.maximum(peak, other_peak)
    far, near_other, other_peak = wave(along_x(near[:n]), swap(near), shift(peak, "z", 2))
    peak = jnp.maximum(peak, other_peak)
    peak = jnp.stack([peak[0, 0], peak[4, 0]])
    far_other, other_peak = wave(swap(far), swap(peak))
    peaks = by_core(core, peak, other_peak).reshape(-1)

    act, normed_two, keep, give = ffn_call(
        at, (pair, near, near_other, far, far_other), cot, gain_rows, w_ffn
    )
    cols = act.shape[2]

    (got,) = wave(swap(give))
    (far,) = wave(sum_far(keep, got))
    ffn_grads = ffn_grad_call(normed_two, cot_flipped, after(act, far))
    near, ffn_grads = wave(sum_near(keep, got, far), ffn_grads)
    ffn_sums = lax.psum_scatter(ffn_grads, ("y", "z"), scatter_dimension=0, tiled=True)
    (rest,) = wave(sum_rest(near))
    dmid = cot_mine.astype(F32) + sum_all(keep, got, near, rest)
    dmid_low = dmid.astype(BF)
    (other,) = wave(swap(dmid_low))
    pair = jnp.concatenate([dmid_low, other], axis=0)
    keep_out, give_out = back_call(at, [(after(act, pair), 2, w_ffn, 2)], None, [], "ffn_out")
    near, give_out = wave(along_x(pair), give_out)
    far, near_other, got_out = wave(along_x(near[:n]), swap(near), swap(give_out))
    (far_other,) = wave(swap(far))
    dattended, proj_grad = proj_call(at, (pair, near, near_other, far, far_other), w_proj, attended)
    dq, dkv = attend_back_call(queries, kv, low, high, lse, dattended, cosine, sine)

    def blocks(v):
        return v.reshape(4, 4, block, -1)

    q_grad = dot(normed_one_t, dq, NN).astype(BF)
    first = blocks(jnp.concatenate([proj_grad, q_grad], axis=1))
    far_0, far_1, first_0, first_1, far_out = wave(
        *reduce_far(dkv, "z", at_z, 1, 1),
        *reduce_far(first, "y", at_y, 0, 2),
        sum_far(keep_out, got_out),
    )
    near_0, near_1, first_0, first_1, near_out = wave(
        *reduce_near(dkv, (far_0, far_1), "z", at_z, 1, 1),
        *reduce_near(first, (first_0, first_1), "y", at_y, 0, 2),
        sum_near(keep_out, got_out, far_out),
    )
    first = total(first, at_y, 0, (first_0, first_1))
    dkv = total(dkv, at_z, 1, (near_0, near_1))
    dprojected, kv_grad = dkv_call(dq, dkv, cosine, sine, normed_one_t)
    keep, give = back_call(at, [(dprojected, 0, w_qkv, 0)], 0, [rows, gain_rows], "qkv_back")
    second = blocks(kv_grad)
    got, first_0, first_1, first_2, far_0, far_1, rest_out = wave(
        swap(give),
        *reduce_direct(first, "z", at_z, 1),
        *reduce_far(second, "z", at_z, 1, 2),
        sum_rest(near_out),
    )
    first = total(first, at_z, 1, (first_0, first_1, first_2)).reshape(block, -1)
    output = mid_mine + sum_all(keep_out, got_out, near_out, rest_out)
    output = swap_blocks(output.astype(BF), 4, 2)[None]

    def rows_of(sums, which):
        both = sums.astype(BF).reshape(2, rows_held, -1)
        return lax.dynamic_index_in_dim(both, which, 0, keepdims=False)

    def whole(sums, other, cols):
        pair = by_core(core, rows_of(sums, core), other)
        parts, start = [], 0
        for n in cols:
            part = pair[:, :, start : start + n]
            parts.append(jnp.concatenate([part[0], part[1]], axis=1).astype(F32))
            start += n
        return parts

    far, near_0, near_1, first_other = wave(
        sum_far(keep, got),
        *reduce_near(second, (far_0, far_1), "z", at_z, 1, 2),
        swap(rows_of(first, 1 - core)),
    )
    second = total(second, at_z, 1, (near_0, near_1))
    near, second_0, second_1, second_2, ffn_sums = wave(
        sum_near(keep, got, far), *reduce_direct(second, "y", at_y, 0), ffn_sums
    )
    second = total(second, at_y, 0, (second_0, second_1, second_2)).reshape(block, -1)
    rest, second_other, ffn_other = wave(
        sum_rest(near), swap(rows_of(second, 1 - core)), swap(rows_of(ffn_sums, 1 - core))
    )
    dinput = dmid + sum_all(keep, got, near, rest)
    input_grad = swap_blocks(dinput, 4, 2)[None]
    gate_part, up_part, down_part = whole(ffn_sums, ffn_other, (cols, cols, cols))
    both = 2 * head_dim
    proj_part, q_part = whole(first, first_other, (both, both))
    (kv_part,) = whole(second, second_other, (both,))
    qkv_part = jnp.concatenate(
        [q_part[:, :both], kv_part[:, :both], q_part[:, both:], kv_part[:, both:]], axis=1
    )

    gain_sums = jnp.stack(
        [
            jnp.sum(qkv_weight.astype(F32) * qkv_part, axis=1),
            jnp.sum(gate_weight.astype(F32) * gate_part, axis=1)
            + jnp.sum(up_weight.astype(F32) * up_part, axis=1),
        ]
    )
    gain_sums = sum(direct(gain_sums, "x"), gain_sums)
    gain_one_grad = gain_sums[0] / attn_gain.astype(F32)
    gain_two_grad = gain_sums[1] / ffn_gain.astype(F32)

    bound = clip_limit[0]
    groups = 2
    factors = jnp.sqrt(bound / jnp.maximum(peaks, bound)).reshape(groups, 2)
    column_scale = jnp.concatenate(
        [factors, jnp.min(factors, axis=1, keepdims=True), jnp.ones((groups, 1), F32)], axis=1
    )
    clipped = (
        qkv_weight.astype(F32).reshape(rows_held, groups, 4, head_dim)
        * column_scale[None, :, :, None]
    ).reshape(rows_held, -1)
    return (
        output,
        input_grad,
        qkv_part,
        proj_part.T,
        gain_one_grad,
        gate_part,
        up_part,
        down_part.T,
        gain_two_grad,
        peaks,
        clipped,
    )


def solution(mesh):
    fine = Mesh(mesh.devices.reshape(4, 2, 4, 4), ("y", "c", "z", "x"))
    rows = ("y", "c", "z")
    act = P(("y", "c"), "z", "x")
    weight = P(rows, "x")
    flipped = P("x", rows)
    return jax.shard_map(
        local,
        mesh=fine,
        in_specs=(
            act, P(("y", "c"), None), P(rows), weight, flipped, P(rows),
            weight, weight, flipped, act, P(),
        ),
        out_specs=(
            act, act, weight, flipped, P(rows), weight, weight, flipped, P(rows), P("x"), weight,
        ),
        check_vma=False,
    )
```

```python
import jax
import jax.numpy as jnp
from jax import lax
from jax.experimental import pallas as pl
from jax.experimental.pallas import tpu as pltpu
from jax.sharding import Mesh
from jax.sharding import PartitionSpec as P

HEAD_DIM = 128
EPS = 1e-05
THETA = 1000000.0
BF = jnp.bfloat16
F32 = jnp.float32
MIB = 1024 * 1024

NN = (((1,), (0,)), ((), ()))
NT = (((1,), (1,)), ((), ()))
TN = (((0,), (0,)), ((), ()))


def dot(a, b, dims):
    return lax.dot_general(a, b, dims, preferred_element_type=F32)


def shape(dims, kind):
    return jax.ShapeDtypeStruct(dims, kind)


def vmem(mib):
    return pltpu.CompilerParams(vmem_limit_bytes=mib * MIB)


def cost(gflop, mib):
    return pl.CostEstimate(
        flops=int(gflop * 1e9), bytes_accessed=int(mib * MIB), transcendentals=0
    )


def shift(v, axis, k):
    n = lax.axis_size(axis)
    return lax.ppermute(v, axis, [(i, (i + k) % n) for i in range(n)])


def swap(v):
    return shift(v, "c", 1)


def column_half(w, which):
    half = w.shape[1] // 2
    return lax.dynamic_slice_in_dim(w, which * half, half, 1)


def by_core(core, own, other):
    return jnp.where(core == 0, jnp.stack([own, other]), jnp.stack([other, own]))


def place(pieces, at, dim):
    own = pieces[0]
    width = own.shape[dim]
    dims = own.shape[:dim] + (4 * width,) + own.shape[dim + 1 :]
    out = jnp.zeros(dims, own.dtype)
    for k, piece in pieces.items():
        out = lax.dynamic_update_slice_in_dim(out, piece, ((at + k) % 4) * width, dim)
    return out


def wave(*arrays):
    return lax.optimization_barrier(arrays)


def after(v, *others):
    return lax.optimization_barrier((v, *others))[0]


def direct(own, axis):
    return shift(own, axis, 1), shift(own, axis, -1), shift(own, axis, 2)


def halves_of(v, cut):
    half = v.shape[cut] // 2
    return lax.slice_in_dim(v, 0, half, axis=cut), lax.slice_in_dim(v, half, 2 * half, axis=cut)


def near_two(own, axis):
    return shift(own, axis, 1), shift(own, axis, -1)


def far_two(before, behind, axis, cut):
    return shift(halves_of(before, cut)[0], axis, 1), shift(halves_of(behind, cut)[1], axis, -1)


def placed(own, near, far, at, dim, cut):
    return place({0: own, -1: near[0], 1: near[1], 2: jnp.concatenate(far, axis=cut)}, at, dim)


def ring_block(v, at, k, dim):
    width = v.shape[dim] // 4
    return lax.dynamic_slice_in_dim(v, ((at + k) % 4) * width, width, dim)


def reduce_far(v, axis, at, dim, cut):
    low, high = halves_of(ring_block(v, at, 2, dim), cut)
    return shift(low, axis, 1), shift(high, axis, -1)


def reduce_near(v, far, axis, at, dim, cut):
    zeros = jnp.zeros_like(far[0])
    up = ring_block(v, at, 1, dim).astype(F32) + jnp.concatenate([far[0], zeros], axis=cut)
    down = ring_block(v, at, -1, dim).astype(F32) + jnp.concatenate([zeros, far[1]], axis=cut)
    return shift(up.astype(BF), axis, 1), shift(down.astype(BF), axis, -1)


def trade(v, axis):
    return lax.all_to_all(v, axis, split_axis=0, concat_axis=0, tiled=True)


def added(v):
    return jnp.sum(v.astype(F32), axis=0)


def total(v, at, dim, parts):
    return sum((p.astype(F32) for p in parts), ring_block(v, at, 0, dim).astype(F32))


def along_x(v):
    return lax.ppermute(
        v, ("c", "x"), [(4 * c + x, 4 * c + (x + 1 - 2 * c) % 4) for c in (0, 1) for x in range(4)]
    )


def sums_kernel(keep_ref, got_ref, far_ref, near_other_ref, near_ref, mine_ref):
    count = far_ref.shape[0]

    def section(k):
        at = pl.ds(k * count, count)
        return keep_ref[at].astype(F32) + got_ref[at].astype(F32)

    far_ref[...] = section(2).astype(BF)
    near_other_ref[...] = section(1).astype(BF)
    near_ref[...] = section(0)
    mine_ref[...] = section(3)


def sums(keep, got):
    rows, width = keep.shape
    part = (rows // 4, width)
    return pl.pallas_call(
        sums_kernel,
        out_shape=[shape(part, BF), shape(part, BF), shape(part, F32), shape(part, F32)],
        compiler_params=vmem(12),
        cost_estimate=cost(0, 6),
        name="sums",
    )(keep, got)


def near_sum(near, far):
    return along_x((near + far.astype(F32)).astype(BF))


def all_sums(mine, near, rest):
    return mine + near.astype(F32) + rest.astype(F32)


def swap_blocks(v, first, second):
    rows = v.shape[0]
    return v.reshape(rows, first, second, -1).swapaxes(1, 2).reshape(rows, -1)


def roll_half(v):
    return pltpu.roll(v, 64, 1)


def lanes(block):
    return pl.ds(pl.multiple_of(block * 512, 512), 512)


def bring(copies, sems, first=0):
    copies = [pltpu.make_async_copy(a, b, sems.at[first + i]) for i, (a, b) in enumerate(copies)]
    for c in copies:
        c.start()
    return copies


def done(copies):
    for c in copies:
        c.wait()


def assembled(at_ref, parts, out_ref):
    count = parts[0].shape[0]
    return [
        (parts[2 * k + i], out_ref.at[pl.ds(i * count, count), lanes(at_ref[k])])
        for k in range(4)
        for i in (0, 1)
    ]


def assembled_rows(at_ref, parts, column, out_ref):
    pair, near, other_near, far, other_far = (
        p.at[:, pl.ds(column * 512, 512)] for p in parts
    )
    count = far.shape[0]
    low, high = pl.ds(0, count), pl.ds(count, count)
    return [
        (pair, out_ref.at[:, lanes(at_ref[0])]),
        (near, out_ref.at[:, lanes(at_ref[1])]),
        (other_near.at[high], out_ref.at[low, lanes(at_ref[2])]),
        (other_near.at[low], out_ref.at[high, lanes(at_ref[2])]),
        (far, out_ref.at[low, lanes(at_ref[3])]),
        (other_far, out_ref.at[high, lanes(at_ref[3])]),
    ]


def far_off(count):
    return [pl.BlockSpec(memory_space=pltpu.HBM)] * count


def fixed(dims):
    return pl.BlockSpec(dims, lambda s, at: (0,) * len(dims))


def call(kernel, at, grid, args, in_specs, out_specs, out_shape, scratch, mib, name, work):
    return pl.pallas_call(
        kernel,
        grid_spec=pltpu.PrefetchScalarGridSpec(
            num_scalar_prefetch=1,
            grid=(grid,),
            in_specs=in_specs,
            out_specs=out_specs,
            scratch_shapes=scratch,
        ),
        out_shape=out_shape,
        compiler_params=vmem(mib),
        cost_estimate=cost(*work),
        name=name,
    )(at, *args)


def qkv_kernel(at_ref, *refs):
    parts, refs = refs[:5], refs[5:]
    gains_ref, w_ref, cos_ref, sin_ref = refs[:4]
    q_ref, kv_ref, nt_ref, row_ref, rows_ref, raw_ref, scale_ref, keep, sems = refs[4:]
    step = pl.program_id(0)
    span = q_ref.shape[0]

    @pl.when(step == 0)
    def _():
        copies = bring(assembled_rows(at_ref, parts, 0, rows_ref), sems)
        keep[...] = gains_ref[...].astype(F32).T[:8]
        row_ref[...] = keep[...]
        done(copies)

    rows = rows_ref[pl.ds(pl.multiple_of(step * span, span), span)].astype(F32)
    scale = lax.rsqrt(jnp.mean(rows * rows, axis=-1, keepdims=True) + EPS)
    normed = (rows * scale * keep[0:1]).astype(BF)
    nt_ref[...] = normed.T
    projected = dot(normed, w_ref[...], NN)
    raw_ref[...] = projected.astype(BF)
    scale_ref[...] = jnp.broadcast_to(scale, scale_ref.shape)
    cosine, sine = cos_ref[...], sin_ref[...]
    out = []
    for i in range(3):
        v = projected[:, i * HEAD_DIM : (i + 1) * HEAD_DIM]
        out.append((v * cosine + roll_half(v) * sine).astype(BF))
    q_ref[...] = jnp.concatenate(out[:2], axis=1)
    kv_ref[0] = jnp.concatenate([out[2], projected[:, 3 * HEAD_DIM :].astype(BF)], axis=1)


def cot_kernel(at_ref, *refs):
    parts, (out_ref, flipped_ref, sems) = refs[:5], refs[5:]
    done(bring(assembled_rows(at_ref, parts, 1, out_ref), sems))
    flipped_ref[...] = out_ref[...].T


def cot_call(at, parts):
    tokens, width = parts[0].shape[0], 4 * 512
    return call(
        cot_kernel,
        at,
        1,
        parts,
        far_off(5),
        [fixed((tokens, width)), fixed((width, tokens))],
        [shape((tokens, width), BF), shape((width, tokens), BF)],
        [pltpu.SemaphoreType.DMA((6,))],
        12,
        "cotangent_rows",
        (0.5, 8),
    )


def qkv_call(at, parts, gains, w_qkv, cosine, sine):
    tokens, (width, cols) = parts[0].shape[0], w_qkv.shape
    span = tokens // 2
    return call(
        qkv_kernel,
        at,
        2,
        (*parts, gains, w_qkv, cosine, sine),
        far_off(5)
        + [
            pl.BlockSpec((width, 128), lambda s, at: (0, 2)),
            fixed((width, cols)),
            fixed((span, HEAD_DIM)),
            fixed((span, HEAD_DIM)),
        ],
        [
            pl.BlockSpec((span, 2 * HEAD_DIM), lambda s, at: (s, 0)),
            pl.BlockSpec((1, span, 2 * HEAD_DIM), lambda s, at: (s, 0, 0)),
            pl.BlockSpec((width, span), lambda s, at: (0, s)),
            fixed((8, width)),
            fixed((tokens, width)),
            pl.BlockSpec((span, cols), lambda s, at: (s, 0)),
            pl.BlockSpec((span, 128), lambda s, at: (s, 0)),
        ],
        [
            shape((tokens, 2 * HEAD_DIM), BF),
            shape((2, span, 2 * HEAD_DIM), BF),
            shape((width, tokens), BF),
            shape((8, width), F32),
            shape((tokens, width), BF),
            shape((tokens, cols), BF),
            shape((tokens, 128), F32),
        ],
        [pltpu.VMEM((8, width), F32), pltpu.SemaphoreType.DMA((6,))],
        12,
        "norm_qkv_rope",
        (2.5, 10),
    )


def stacked(v):
    return jnp.concatenate([v[:, :HEAD_DIM], v[:, HEAD_DIM:]], axis=0)


def allowed_mask(low_ref, high_ref, length):
    low, high = low_ref[0], high_ref[...]
    places = lax.broadcasted_iota(jnp.int32, (length, low.shape[1]), 0)
    mask = (places >= low) & (places <= high)
    return jnp.concatenate([mask, mask], axis=1)


def attend_kernel(q_ref, kv_ref, low_ref, high_ref, out_ref, lse_ref, peak_ref):
    length = kv_ref.shape[1]
    span = q_ref.shape[0]
    queries = stacked(q_ref[...])
    keys, values = kv_ref[0, :, :HEAD_DIM], kv_ref[0, :, HEAD_DIM:]
    raw = dot(keys, queries, NT)
    scores = jnp.where(allowed_mask(low_ref, high_ref, length), raw * HEAD_DIM**-0.5, -1e30)
    largest = jnp.max(scores, axis=0, keepdims=True)
    weights = jnp.exp(scores - largest)
    total = jnp.sum(weights, axis=0, keepdims=True)
    probs = (weights * (1.0 / total)).astype(BF)
    attended = dot(values, probs, TN).T.astype(BF)
    out_ref[...] = jnp.concatenate([attended[:span], attended[span:]], axis=1)
    lse_ref[0] = largest + jnp.log(total)
    tops = [jnp.max(largest[:, h * span : (h + 1) * span], axis=1, keepdims=True) for h in (0, 1)]
    peak_ref[0] = jnp.concatenate([jnp.broadcast_to(t, (4, 128)) for t in tops], axis=0)


def attend_call(queries, kv, low, high):
    tokens = queries.shape[0]
    span, length, both = tokens // 2, kv.shape[1], 2 * HEAD_DIM
    return pl.pallas_call(
        attend_kernel,
        grid=(2,),
        in_specs=[
            pl.BlockSpec((span, both), lambda s: (s, 0)),
            pl.BlockSpec((1, length, both), lambda s: (s, 0, 0)),
            pl.BlockSpec((1, 1, span), lambda s: (s, 0, 0)),
            pl.BlockSpec((1, span), lambda s: (0, 0)),
        ],
        out_specs=[
            pl.BlockSpec((span, both), lambda s: (s, 0)),
            pl.BlockSpec((1, 1, 2 * span), lambda s: (s, 0, 0)),
            pl.BlockSpec((1, 8, 128), lambda s: (s, 0, 0)),
        ],
        out_shape=[
            shape((tokens, both), BF),
            shape((2, 1, 2 * span), F32),
            shape((2, 8, 128), F32),
        ],
        compiler_params=vmem(8),
        cost_estimate=cost(2.5, 4),
        name="attend",
    )(queries, kv, low, high)


def attend_back_kernel(
    q_ref, kv_ref, low_ref, high_ref, lse_ref, up_ref, cos_ref, sin_ref, dq_ref, dkv_ref
):
    length = kv_ref.shape[1]
    span = q_ref.shape[0]
    queries, upstream = stacked(q_ref[...]), stacked(up_ref[...])
    keys, values = kv_ref[0, :, :HEAD_DIM], kv_ref[0, :, HEAD_DIM:]
    raw = dot(keys, queries, NT)
    factor = HEAD_DIM**-0.5
    probs = jnp.where(
        allowed_mask(low_ref, high_ref, length), jnp.exp(raw * factor - lse_ref[0]), 0.0
    )
    dprobs = dot(values, upstream, NT)
    rowdot = jnp.sum(probs * dprobs, axis=0, keepdims=True)
    dscores = (probs * (dprobs - rowdot) * factor).astype(BF)
    dkey = dot(dscores, queries, NN)
    dvalue = dot(probs.astype(BF), upstream, NN)
    dkv_ref[0] = jnp.concatenate([dkey, dvalue], axis=1).astype(BF)
    dquery = dot(keys, dscores, TN).T
    cosine, sine = cos_ref[...], sin_ref[...]
    heads = []
    for h in (0, 1):
        d = dquery[h * span : (h + 1) * span]
        heads.append((d * cosine - roll_half(d) * sine).astype(BF))
    dq_ref[...] = jnp.concatenate(heads, axis=1)


def attend_back_call(queries, kv, low, high, lse, upstream, cosine, sine):
    tokens = queries.shape[0]
    span, length, both = tokens // 2, kv.shape[1], 2 * HEAD_DIM
    table = pl.BlockSpec((span, HEAD_DIM), lambda s: (0, 0))
    return pl.pallas_call(
        attend_back_kernel,
        grid=(2,),
        in_specs=[
            pl.BlockSpec((span, both), lambda s: (s, 0)),
            pl.BlockSpec((1, length, both), lambda s: (s, 0, 0)),
            pl.BlockSpec((1, 1, span), lambda s: (s, 0, 0)),
            pl.BlockSpec((1, span), lambda s: (0, 0)),
            pl.BlockSpec((1, 1, 2 * span), lambda s: (s, 0, 0)),
            pl.BlockSpec((span, both), lambda s: (s, 0)),
            table,
            table,
        ],
        out_specs=[
            pl.BlockSpec((span, both), lambda s: (s, 0)),
            pl.BlockSpec((1, length, both), lambda s: (s, 0, 0)),
        ],
        out_shape=[shape((tokens, both), BF), shape((2, length, both), BF)],
        compiler_params=vmem(10),
        cost_estimate=cost(4.5, 4),
        name="attend_back",
    )(queries, kv, low, high, lse, upstream, cosine, sine)


def ffn_kernel(at_ref, *refs):
    parts, refs = refs[:8], refs[8:]
    cot_hbm, cot_t_hbm, gain_hbm, wg_ref, wu_ref, wd_ref = refs[:6]
    act_ref, grad_ref, mid_ref, stat_ref = refs[6:10]
    normed_ref, flipped_ref, cot_ref, cot_t_ref, gain_ref, sems = refs[10:]
    step = pl.program_id(0)

    @pl.when(step == 0)
    def _():
        copies = [(gain_hbm, gain_ref), *assembled(at_ref, parts, mid_ref)]
        copies = bring(copies + [(cot_hbm, cot_ref), (cot_t_hbm, cot_t_ref)], sems)
        done(copies[:-2])

        @pl.loop(0, mid_ref.shape[0] // 128)
        def _(i):
            rows = pl.ds(pl.multiple_of(i * 128, 128), 128)
            mid = mid_ref[rows].astype(F32)
            scale = lax.rsqrt(jnp.mean(mid * mid, axis=-1, keepdims=True) + EPS)
            normed = (mid * scale * gain_ref[1:2]).astype(BF)
            normed_ref[rows] = normed
            flipped_ref[:, rows] = normed.T
            stat_ref[0, rows] = jnp.zeros((128, 128), F32)
            stat_ref[1, rows] = jnp.broadcast_to(scale, (128, 128))

        done(copies[-2:])

    normed = normed_ref[...]
    gate = dot(normed, wg_ref[...], NN)
    upper = dot(normed, wu_ref[...], NN)
    dhidden = dot(cot_ref[...], wd_ref[...], NN)
    sigmoid = 1.0 / (1.0 + jnp.exp(-gate))
    silu = gate * sigmoid
    slope = sigmoid * (1.0 + gate * (1.0 - sigmoid))
    dgate = (dhidden * upper * slope).astype(BF)
    dupper = (dhidden * silu).astype(BF)
    hidden = (silu * upper).astype(BF)
    act_ref[0] = dgate
    act_ref[1] = dupper
    act_ref[2] = hidden
    inner = jnp.sum(dgate.astype(F32) * gate + dupper.astype(F32) * upper, axis=-1, keepdims=True)
    stat_ref[0] += jnp.broadcast_to(inner, stat_ref.shape[1:])
    flipped = flipped_ref[...]
    for i, (left, right) in enumerate(((flipped, dgate), (flipped, dupper), (cot_t_ref[...], hidden))):
        grad = dot(left, right, NN).astype(BF)
        grad_ref[:, i] = grad.reshape(16, grad.shape[0] // 16, grad.shape[1])


def ffn_call(at, mid_parts, cot, cot_flipped, gains, w):
    tokens, width = cot.shape
    cols = w.shape[1] // 3
    block = 512
    steps = cols // block

    def columns(i):
        return pl.BlockSpec((width, block), lambda j, at: (0, i * steps + j))

    return call(
        ffn_kernel,
        at,
        steps,
        (*mid_parts, cot, cot_flipped, gains, w, w, w),
        far_off(11) + [columns(0), columns(1), columns(2)],
        [
            pl.BlockSpec((3, tokens, block), lambda j, at: (0, 0, j)),
            pl.BlockSpec((16, 3, width // 16, block), lambda j, at: (0, 0, 0, j)),
            fixed((tokens, width)),
            fixed((2, tokens, 128)),
        ],
        [
            shape((3, tokens, cols), BF),
            shape((16, 3, width // 16, cols), BF),
            shape((tokens, width), BF),
            shape((2, tokens, 128), F32),
        ],
        [
            pltpu.VMEM((tokens, width), BF),
            pltpu.VMEM((width, tokens), BF),
            pltpu.VMEM((tokens, width), BF),
            pltpu.VMEM((width, tokens), BF),
            pltpu.VMEM((8, width), F32),
            pltpu.SemaphoreType.DMA((11,)),
        ],
        60,
        "ffn",
        (16, 40),
    )


def norm_back(v, base, gain, stat):
    inner, scale = stat[0, :, 0:1], stat[1, :, 0:1]
    factor = scale * scale * inner / (4 * v.shape[1])
    return scale * (gain * v) - base.astype(F32) * factor


def send_order(v, step, keep_ref, give_ref):
    v = v.astype(BF)
    count = v.shape[0] // 2

    @pl.when(step == 0)
    def _():
        keep_ref[: 2 * count] = v

    @pl.when(step == 1)
    def _():
        give_ref[:count] = v[count:]
        give_ref[count : 2 * count] = v[:count]

    @pl.when(step >= 2)
    def _():
        at = pl.ds(pl.multiple_of(step * count, count), count)
        keep_ref[at] = v[:count]
        give_ref[at] = v[count:]


def back_kernel(terms, norm, at_ref, *refs):
    a_refs, w_refs, refs = refs[:terms], refs[terms : 2 * terms], refs[2 * terms :]
    v = sum(dot(a[0], w[...], NT) for a, w in zip(a_refs, w_refs))
    if norm is not None:
        base_ref, gain_ref, stat_ref, *refs = refs
        v = norm_back(v, base_ref[...], gain_ref[norm : norm + 1], stat_ref)
    if len(refs) == 4:
        block, beside, refs = v.shape[1], refs[:2], refs[2:]

        @pl.when(pl.program_id(0) == 0)
        def _():
            refs[0][:, block:] = beside[0][...]
            refs[1][:, block:] = beside[1][...]

        refs = [r.at[:, pl.ds(0, block)] for r in refs]
    send_order(v, pl.program_id(0), *refs)


def back_call(at, pairs, norm, extra, name, mib=12, beside=()):
    tokens, width = pairs[0][0].shape[1], pairs[0][2].shape[0]
    block = width // 4
    args, specs = [], []
    for a, i, _, _ in pairs:
        args.append(a)
        specs.append(pl.BlockSpec((1, tokens, a.shape[2]), lambda s, at, i=i: (i, 0, 0)))
    for a, _, w, j in pairs:
        args.append(w)
        specs.append(pl.BlockSpec((block, a.shape[2]), lambda s, at, j=j: (at[4 + s], j)))
    if norm is not None:
        args += extra
        specs += [
            pl.BlockSpec((tokens, block), lambda s, at: (0, at[4 + s])),
            pl.BlockSpec((8, block), lambda s, at: (0, at[4 + s])),
            fixed((2, tokens, 128)),
        ]
    args += beside
    specs += [fixed((2 * tokens, block)) for _ in beside]
    moved = (2 * tokens, 2 * block if beside else block)

    def kernel(*refs):
        back_kernel(len(pairs), norm, *refs)

    return call(
        kernel,
        at,
        4,
        args,
        specs,
        [fixed(moved)] * 2,
        [shape(moved, BF)] * 2,
        [],
        mib,
        name,
        (sum(1.2e-9 * 2 * tokens * width * a.shape[2] for a, *_ in pairs) + 1, 8),
    )


def proj_kernel(at_ref, *refs):
    parts, (w_ref, datt_ref, up_ref, sems) = refs[:8], refs[8:]
    done(bring(assembled(at_ref, parts, up_ref), sems))
    datt_ref[...] = dot(up_ref[...], w_ref[...], NN).astype(BF)


def proj_call(at, parts, w_proj, cols):
    tokens, width = 2 * parts[0].shape[0], w_proj.shape[0]
    return call(
        proj_kernel,
        at,
        1,
        (*parts, w_proj),
        far_off(8) + [fixed((width, cols))],
        [fixed((tokens, cols)), fixed((tokens, width))],
        [shape((tokens, cols), BF), shape((tokens, width), BF)],
        [pltpu.SemaphoreType.DMA((8,))],
        60,
        "proj_back",
        (1.5, 6),
    )


def proj_grad_kernel(up_ref, att_ref, grad_ref):
    grad_ref[...] = dot(att_ref[...], up_ref[...], TN).T.astype(BF)


def proj_grad_call(up, attended):
    return pl.pallas_call(
        proj_grad_kernel,
        out_shape=shape((up.shape[1], attended.shape[1]), BF),
        compiler_params=vmem(24),
        cost_estimate=cost(2, 4),
        name="proj_grad",
    )(up, attended)


def dkv_kernel(
    dq_ref, dkv_ref, near_ref, far_ref, raw_ref, scale_ref, cos_ref, sin_ref, nt_ref, proj_ref,
    d_ref, grad_ref, stat_ref,
):
    span = dkv_ref.shape[1]
    both = 2 * HEAD_DIM
    cosine, sine = cos_ref[...], sin_ref[...]
    d_ref[0, :, :both] = dq_ref[...]
    for s in (0, 1):
        dkv = sum(r[s].astype(F32) for r in (dkv_ref, near_ref, far_ref))
        dk = dkv[:, :HEAD_DIM]
        at = pl.ds(s * span, span)
        d_ref[0, at, both : 3 * HEAD_DIM] = (dk * cosine - roll_half(dk) * sine).astype(BF)
        d_ref[0, at, 3 * HEAD_DIM :] = dkv[:, HEAD_DIM:].astype(BF)
    d = d_ref[0]
    inner = jnp.sum(d.astype(F32) * raw_ref[...].astype(F32), axis=-1, keepdims=True)
    stat_ref[0] = jnp.broadcast_to(inner, stat_ref.shape[1:])
    stat_ref[1] = scale_ref[...]
    grad_ref[:, :both] = proj_ref[...]
    grad_ref[:, both:] = dot(nt_ref[...], d, NN).astype(BF)


def dkv_call(dq, dkv, near, far, raw, scale, cosine, sine, nt, proj_grad):
    tokens, width = dq.shape[0], nt.shape[0]
    both = 2 * HEAD_DIM
    return pl.pallas_call(
        dkv_kernel,
        out_shape=[
            shape((1, tokens, 2 * both), BF),
            shape((width, 3 * both), BF),
            shape((2, tokens, 128), F32),
        ],
        compiler_params=vmem(8),
        cost_estimate=cost(2, 8),
        name="dqkv",
    )(dq, dkv, near, far, raw, scale, cosine, sine, nt, proj_grad)


def local(
    activations,
    segment_ids,
    attn_gain,
    qkv_weight,
    proj_weight,
    ffn_gain,
    gate_weight,
    up_weight,
    down_weight,
    cotangent,
    clip_limit,
):
    core = lax.axis_index("c")
    at_x = lax.axis_index("x")
    at_y = lax.axis_index("y")
    at_z = lax.axis_index("z")
    _, span, width = activations.shape
    head_dim = HEAD_DIM
    rows_held = qkv_weight.shape[0]
    block = 2 * rows_held

    side = 1 - 2 * core
    at = [at_x, at_x - side, at_x + side, at_x + 2]
    at = jnp.stack(at + [at[2], at[1], at[3], at[0]]).astype(jnp.int32) % 4

    gains = jnp.concatenate(
        [attn_gain[:, None], ffn_gain[:, None], jnp.zeros((rows_held, 126), BF)], axis=1
    )

    def halves(parts, extra):
        own = jnp.concatenate([column_half(w, core) for w in parts] + extra, axis=1)
        away = jnp.concatenate([column_half(w, 1 - core) for w in parts] + extra, axis=1)
        return own, away

    def both_rows(own, other):
        return by_core(core, own, other).reshape(block, -1)

    rows_mine = swap_blocks(activations[0], 2, 4)
    cot_mine = swap_blocks(cotangent[0], 2, 4)
    own_rows = jnp.concatenate([rows_mine, cot_mine], axis=1)
    attn_own, attn_away = halves((qkv_weight, proj_weight.T), [gains])
    ffn_own, ffn_away = halves((gate_weight, up_weight, down_weight.T), [])
    attn_other, rows_other, ids_other = wave(swap(attn_away), swap(own_rows), swap(segment_ids))
    attn_shard = both_rows(attn_own, attn_other)
    a0, b0 = attn_shard[None, :, : 4 * head_dim], attn_shard[None, :, 4 * head_dim :]
    pair = jnp.concatenate([own_rows, rows_other], axis=0)

    *got, row_near, ffn_other = wave(
        *direct(a0, "y"), *direct(b0, "z"), along_x(pair), swap(ffn_away)
    )
    a1 = place(dict(zip((0, -1, 1, 2), (a0, *got[:3]))), at_y, 0)[:, None]
    b1 = place(dict(zip((0, -1, 1, 2), (b0, *got[3:]))), at_z, 0)[None]
    *got, row_far, row_near_other = wave(
        *near_two(a1, "z"), *near_two(b1, "y"), along_x(row_near[:span]), swap(row_near)
    )
    a_near, b_near = got[:2], got[2:]
    row_far_other = swap(row_far)
    ffn_shard = both_rows(ffn_own, after(ffn_other, a_near[0]))
    w_ffn = lax.all_gather(ffn_shard, ("y", "z"), axis=0, tiled=True)
    a_far_0, a_far_1, b_far_0, b_far_1, row_far_other = wave(
        *far_two(*a_near, "z", 2), *far_two(*b_near, "y", 2), row_far_other
    )

    def in_rows(v):
        return v.reshape(16 * block, -1)

    w_qkv = in_rows(placed(a1, a_near, (a_far_0, a_far_1), at_z, 1, 2))
    w_proj = in_rows(placed(b1, b_near, (b_far_0, b_far_1), at_y, 0, 2))
    row_parts = (pair, row_near, row_near_other, row_far, row_far_other)

    half = head_dim // 2
    freqs = 1.0 / THETA ** (jnp.arange(half, dtype=F32) * 2.0 / head_dim)
    places = at_z * span + jnp.arange(span)
    angles = places.astype(F32)[:, None] * freqs[None, :]
    cosine = jnp.cos(jnp.concatenate([angles, angles], axis=1))
    sine = jnp.sin(angles)
    sine = jnp.concatenate([-sine, sine], axis=1)
    ids = jnp.concatenate([segment_ids, ids_other], axis=0)
    query_ids = lax.dynamic_slice_in_dim(ids, at_z * span, span, 1)
    low = jnp.sum(ids[:, :, None] < query_ids[:, None, :], axis=1, dtype=jnp.int32)[:, None, :]
    high = places.astype(jnp.int32)[None, :]

    queries, kv_mine, normed_one_t, gain_rows, rows, raw, scale_one = qkv_call(
        at, row_parts, w_proj, w_qkv, cosine, sine
    )
    kv_near = wave(*near_two(kv_mine, "z"))
    cot, cot_flipped = cot_call(at, (after(pair, kv_near[0]), *row_parts[1:]))
    *kv_far, cot, cot_flipped = wave(*far_two(*kv_near, "z", 1), cot, cot_flipped)
    kv = placed(kv_mine, kv_near, kv_far, at_z, 1, 1)
    attended, lse, peak = attend_call(queries, kv, low, high)
    peak = jnp.max(peak, axis=0)
    keep, give = back_call(at, [(attended[None], 0, w_proj, 0)], None, [], "branch")

    (got,) = wave(swap(give))
    far, near_other, near, mine = sums(keep, got)
    near_other = along_x(near_other)
    far, other_peak = wave(along_x(far), shift(peak, "y", 1))
    peak = jnp.maximum(peak, other_peak)
    near, rest, other_peak = wave(near_sum(near, far), swap(near_other), shift(peak, "y", 2))
    peak = jnp.maximum(peak, other_peak)
    mid_mine = rows_mine.astype(F32) + all_sums(mine, near, rest)
    own = mid_mine.astype(BF)
    other = swap(own)
    near_other = along_x(other)
    near, other_peak = wave(along_x(own), shift(peak, "z", 1))
    peak = jnp.maximum(peak, other_peak)
    far, near_other, near_swap, other_peak = wave(
        along_x(near), near_other, swap(near), shift(peak, "z", 2)
    )
    peak = jnp.maximum(peak, other_peak)
    peak = jnp.stack([peak[0, 0], peak[4, 0]])
    far_swap, near_other_swap, other_peak = wave(swap(far), swap(near_other), swap(peak))
    peaks = by_core(core, peak, other_peak).reshape(-1)
    mid_parts = (own, other, near, near_other, near_other_swap, near_swap, far, far_swap)

    act, ffn_grads, mid, stat = ffn_call(at, mid_parts, cot, cot_flipped, gain_rows, w_ffn)
    ffn_sums = lax.psum_scatter(ffn_grads, ("y", "z"), scatter_dimension=0, tiled=True)
    keep, give = back_call(
        at, [(act, 0, w_ffn, 0), (act, 1, w_ffn, 1)], 1, [mid, gain_rows, stat], "ffn_back", 60
    )

    (got,) = wave(swap(give))
    far, near_other, near, mine = sums(keep, got)
    near_other = along_x(near_other)
    keep_out, give_out = back_call(
        at, [(after(act, far), 2, w_ffn, 2)], None, [], "ffn_out", 60
    )
    far, keep_out, give_out = wave(along_x(far), keep_out, give_out)
    near, rest = wave(near_sum(near, far), swap(near_other))
    dmid = cot_mine.astype(F32) + all_sums(mine, near, rest)
    own = dmid.astype(BF)
    other = swap(own)
    near_other = along_x(other)
    (near,) = wave(along_x(own))
    far, near_other, near_swap = wave(along_x(near), near_other, swap(near))
    far_swap, near_other_swap = wave(swap(far), swap(near_other))
    dmid_parts = (own, other, near, near_other, near_other_swap, near_swap, far, far_swap)
    dattended, up = proj_call(at, dmid_parts, w_proj, attended.shape[1])
    dq, dkv = attend_back_call(queries, kv, low, high, lse, dattended, cosine, sine)

    far_0, far_1 = wave(*reduce_far(dkv, "z", at_z, 1, 1))
    proj_grad = proj_grad_call(after(up, far_0), attended)
    near_0, near_1, proj_grad = wave(*reduce_near(dkv, (far_0, far_1), "z", at_z, 1, 1), proj_grad)
    dprojected, attn_grads, stat = dkv_call(
        dq, ring_block(dkv, at_z, 0, 1), near_0, near_1, raw, scale_one, cosine, sine,
        normed_one_t, proj_grad,
    )
    attn_sums = trade(attn_grads.reshape(16, block, -1), ("y", "z"))
    keep, give = back_call(
        at, [(dprojected, 0, w_qkv, 0)], 0, [rows, gain_rows, stat], "qkv_back", 12,
        (keep_out, give_out),
    )
    got, ffn_sums = wave(swap(give), ffn_sums)
    far, near_other, near, mine = sums(keep, got)
    near_other = along_x(near_other)

    def rows_of(sums, which):
        both = sums.astype(BF).reshape(-1, 2, rows_held, sums.shape[-1])
        return lax.dynamic_index_in_dim(both, which, 1, keepdims=False)

    def whole(own, other):
        return jnp.concatenate(list(by_core(core, own, other)), axis=1).astype(F32)

    far, ffn_other = wave(along_x(far), swap(rows_of(ffn_sums, 1 - core)))
    own = rows_of(ffn_sums, core)
    gate_part, up_part, down_part = (whole(own[i], ffn_other[i]) for i in range(3))
    gain_two_sum = jnp.sum(gate_weight.astype(F32) * gate_part, axis=1) + jnp.sum(
        up_weight.astype(F32) * up_part, axis=1
    )
    near, rest, attn_sums, gate_part, up_part, down_part, gain_two_sum = wave(
        near_sum(near, far), swap(near_other), attn_sums,
        gate_part, up_part, down_part, gain_two_sum,
    )
    in_sums = all_sums(mine, near, rest)
    input_grad = swap_blocks(dmid + in_sums[:, :width], 4, 2)[None]
    output = swap_blocks((mid_mine + in_sums[:, width:]).astype(BF), 4, 2)[None]
    attn_sums = added(attn_sums)
    other = swap(rows_of(attn_sums, 1 - core))[0]
    both = 2 * head_dim
    own = rows_of(attn_sums, core)[0]
    proj_part = whole(own[:, :both], other[:, :both])
    qkv_part = whole(own[:, both:], other[:, both:])

    gain_sums = jnp.stack([jnp.sum(qkv_weight.astype(F32) * qkv_part, axis=1), gain_two_sum])
    gain_sums = sum(direct(gain_sums, "x"), gain_sums)
    gain_one_grad = gain_sums[0] / attn_gain.astype(F32)
    gain_two_grad = gain_sums[1] / ffn_gain.astype(F32)

    bound = clip_limit[0]
    groups = 2
    factors = jnp.sqrt(bound / jnp.maximum(peaks, bound)).reshape(groups, 2)
    column_scale = jnp.concatenate(
        [factors, jnp.min(factors, axis=1, keepdims=True), jnp.ones((groups, 1), F32)], axis=1
    )
    clipped = (
        qkv_weight.astype(F32).reshape(rows_held, groups, 4, head_dim)
        * column_scale[None, :, :, None]
    ).reshape(rows_held, -1)
    return (
        output,
        input_grad,
        qkv_part,
        proj_part.T,
        gain_one_grad,
        gate_part,
        up_part,
        down_part.T,
        gain_two_grad,
        peaks,
        clipped,
    )


def solution(mesh):
    fine = Mesh(mesh.devices.reshape(4, 2, 4, 4), ("y", "c", "z", "x"))
    rows = ("y", "c", "z")
    act = P(("y", "c"), "z", "x")
    weight = P(rows, "x")
    flipped = P("x", rows)
    return jax.shard_map(
        local,
        mesh=fine,
        in_specs=(
            act, P(("y", "c"), None), P(rows), weight, flipped, P(rows),
            weight, weight, flipped, act, P(),
        ),
        out_specs=(
            act, act, weight, flipped, P(rows), weight, weight, flipped, P(rows), P("x"), weight,
        ),
        check_vma=False,
    )
```

```python
import jax
import jax.numpy as jnp
from jax import lax
from jax.experimental import pallas as pl
from jax.experimental.pallas import tpu as pltpu
from jax.sharding import Mesh
from jax.sharding import PartitionSpec as P

HEAD_DIM = 128
EPS = 1e-05
THETA = 1000000.0
BF = jnp.bfloat16
F32 = jnp.float32
MIB = 1024 * 1024

NN = (((1,), (0,)), ((), ()))
NT = (((1,), (1,)), ((), ()))
TN = (((0,), (0,)), ((), ()))


def dot(a, b, dims):
    return lax.dot_general(a, b, dims, preferred_element_type=F32)


def shape(dims, kind):
    return jax.ShapeDtypeStruct(dims, kind)


def vmem(mib):
    return pltpu.CompilerParams(vmem_limit_bytes=mib * MIB)


def cost(gflop, mib):
    return pl.CostEstimate(
        flops=int(gflop * 1e9), bytes_accessed=int(mib * MIB), transcendentals=0
    )


def shift(v, axis, k):
    n = lax.axis_size(axis)
    return lax.ppermute(v, axis, [(i, (i + k) % n) for i in range(n)])


def swap(v):
    return shift(v, "c", 1)


def column_half(w, which):
    half = w.shape[1] // 2
    return lax.dynamic_slice_in_dim(w, which * half, half, 1)


def by_core(core, own, other):
    return jnp.where(core == 0, jnp.stack([own, other]), jnp.stack([other, own]))


def place(pieces, at, dim):
    own = pieces[0]
    width = own.shape[dim]
    dims = own.shape[:dim] + (4 * width,) + own.shape[dim + 1 :]
    out = jnp.zeros(dims, own.dtype)
    for k, piece in pieces.items():
        out = lax.dynamic_update_slice_in_dim(out, piece, ((at + k) % 4) * width, dim)
    return out


def wave(*arrays):
    return lax.optimization_barrier(arrays)


def after(v, *others):
    return lax.optimization_barrier((v, *others))[0]


def direct(own, axis):
    return shift(own, axis, 1), shift(own, axis, -1), shift(own, axis, 2)


def halves_of(v, cut):
    half = v.shape[cut] // 2
    return lax.slice_in_dim(v, 0, half, axis=cut), lax.slice_in_dim(v, half, 2 * half, axis=cut)


def near_two(own, axis):
    return shift(own, axis, 1), shift(own, axis, -1)


def far_two(before, behind, axis, cut):
    return shift(halves_of(before, cut)[0], axis, 1), shift(halves_of(behind, cut)[1], axis, -1)


def placed(own, near, far, at, dim, cut):
    return place({0: own, -1: near[0], 1: near[1], 2: jnp.concatenate(far, axis=cut)}, at, dim)


def ring_block(v, at, k, dim):
    width = v.shape[dim] // 4
    return lax.dynamic_slice_in_dim(v, ((at + k) % 4) * width, width, dim)


def reduce_far(v, axis, at, dim, cut):
    low, high = halves_of(ring_block(v, at, 2, dim), cut)
    return shift(low, axis, 1), shift(high, axis, -1)


def reduce_near(v, far, axis, at, dim, cut):
    zeros = jnp.zeros_like(far[0])
    up = ring_block(v, at, 1, dim).astype(F32) + jnp.concatenate([far[0], zeros], axis=cut)
    down = ring_block(v, at, -1, dim).astype(F32) + jnp.concatenate([zeros, far[1]], axis=cut)
    return shift(up.astype(BF), axis, 1), shift(down.astype(BF), axis, -1)


def trade(v, axis):
    return lax.all_to_all(v, axis, split_axis=0, concat_axis=0, tiled=True)


def added(v):
    return jnp.sum(v.astype(F32), axis=0)


def total(v, at, dim, parts):
    return sum((p.astype(F32) for p in parts), ring_block(v, at, 0, dim).astype(F32))


def along_x(v):
    return lax.ppermute(
        v, ("c", "x"), [(4 * c + x, 4 * c + (x + 1 - 2 * c) % 4) for c in (0, 1) for x in range(4)]
    )


def sums_kernel(keep_ref, got_ref, far_ref, near_other_ref, near_ref, mine_ref):
    count = far_ref.shape[0]

    def section(k):
        at = pl.ds(k * count, count)
        return keep_ref[at].astype(F32) + got_ref[at].astype(F32)

    far_ref[...] = section(2).astype(BF)
    near_other_ref[...] = section(1).astype(BF)
    near_ref[...] = section(0)
    mine_ref[...] = section(3)


def sums(keep, got):
    rows, width = keep.shape
    part = (rows // 4, width)
    return pl.pallas_call(
        sums_kernel,
        out_shape=[shape(part, BF), shape(part, BF), shape(part, F32), shape(part, F32)],
        compiler_params=vmem(12),
        cost_estimate=cost(0, 6),
        name="sums",
    )(keep, got)


def near_sum(near, far):
    return along_x((near + far.astype(F32)).astype(BF))


def all_sums(mine, near, rest):
    return mine + near.astype(F32) + rest.astype(F32)


def swap_blocks(v, first, second):
    rows = v.shape[0]
    return v.reshape(rows, first, second, -1).swapaxes(1, 2).reshape(rows, -1)


def roll_half(v):
    return pltpu.roll(v, 64, 1)


def lanes(block):
    return pl.ds(pl.multiple_of(block * 512, 512), 512)


def bring(copies, sems, first=0):
    copies = [pltpu.make_async_copy(a, b, sems.at[first + i]) for i, (a, b) in enumerate(copies)]
    for c in copies:
        c.start()
    return copies


def done(copies):
    for c in copies:
        c.wait()


def assembled(at_ref, parts, out_ref):
    count = parts[0].shape[0]
    return [
        (parts[2 * k + i], out_ref.at[pl.ds(i * count, count), lanes(at_ref[k])])
        for k in range(4)
        for i in (0, 1)
    ]


def assembled_rows(at_ref, parts, column, out_ref):
    pair, near, other_near, far, other_far = (
        p.at[:, pl.ds(column * 512, 512)] for p in parts
    )
    count = far.shape[0]
    low, high = pl.ds(0, count), pl.ds(count, count)
    return [
        (pair, out_ref.at[:, lanes(at_ref[0])]),
        (near, out_ref.at[:, lanes(at_ref[1])]),
        (other_near.at[high], out_ref.at[low, lanes(at_ref[2])]),
        (other_near.at[low], out_ref.at[high, lanes(at_ref[2])]),
        (far, out_ref.at[low, lanes(at_ref[3])]),
        (other_far, out_ref.at[high, lanes(at_ref[3])]),
    ]


def far_off(count):
    return [pl.BlockSpec(memory_space=pltpu.HBM)] * count


def fixed(dims):
    return pl.BlockSpec(dims, lambda s, at: (0,) * len(dims))


def call(kernel, at, grid, args, in_specs, out_specs, out_shape, scratch, mib, name, work):
    return pl.pallas_call(
        kernel,
        grid_spec=pltpu.PrefetchScalarGridSpec(
            num_scalar_prefetch=1,
            grid=(grid,),
            in_specs=in_specs,
            out_specs=out_specs,
            scratch_shapes=scratch,
        ),
        out_shape=out_shape,
        compiler_params=vmem(mib),
        cost_estimate=cost(*work),
        name=name,
    )(at, *args)


def qkv_kernel(at_ref, *refs):
    parts, refs = refs[:5], refs[5:]
    gains_ref, w_ref, cos_ref, sin_ref = refs[:4]
    q_ref, kv_ref, nt_ref, row_ref, rows_ref, raw_ref, scale_ref, keep, sems = refs[4:]
    step = pl.program_id(0)
    span = q_ref.shape[0]

    @pl.when(step == 0)
    def _():
        copies = bring(assembled_rows(at_ref, parts, 0, rows_ref), sems)
        keep[...] = gains_ref[...].astype(F32).T[:8]
        row_ref[...] = keep[...]
        done(copies)

    rows = rows_ref[pl.ds(pl.multiple_of(step * span, span), span)].astype(F32)
    scale = lax.rsqrt(jnp.mean(rows * rows, axis=-1, keepdims=True) + EPS)
    normed = (rows * scale * keep[0:1]).astype(BF)
    nt_ref[...] = normed.T
    projected = dot(normed, w_ref[...], NN)
    raw_ref[...] = projected.astype(BF)
    scale_ref[...] = jnp.broadcast_to(scale, scale_ref.shape)
    cosine, sine = cos_ref[...], sin_ref[...]
    out = []
    for i in range(3):
        v = projected[:, i * HEAD_DIM : (i + 1) * HEAD_DIM]
        out.append((v * cosine + roll_half(v) * sine).astype(BF))
    q_ref[...] = jnp.concatenate(out[:2], axis=1)
    kv_ref[0] = jnp.concatenate([out[2], projected[:, 3 * HEAD_DIM :].astype(BF)], axis=1)


def cot_kernel(at_ref, *refs):
    parts, (out_ref, flipped_ref, sems) = refs[:5], refs[5:]
    done(bring(assembled_rows(at_ref, parts, 1, out_ref), sems))
    flipped_ref[...] = out_ref[...].T


def cot_call(at, parts):
    tokens, width = parts[0].shape[0], 4 * 512
    return call(
        cot_kernel,
        at,
        1,
        parts,
        far_off(5),
        [fixed((tokens, width)), fixed((width, tokens))],
        [shape((tokens, width), BF), shape((width, tokens), BF)],
        [pltpu.SemaphoreType.DMA((6,))],
        12,
        "cotangent_rows",
        (0.5, 8),
    )


def qkv_call(at, parts, gains, w_qkv, cosine, sine):
    tokens, (width, cols) = parts[0].shape[0], w_qkv.shape
    span = tokens // 2
    return call(
        qkv_kernel,
        at,
        2,
        (*parts, gains, w_qkv, cosine, sine),
        far_off(5)
        + [
            pl.BlockSpec((width, 128), lambda s, at: (0, 2)),
            fixed((width, cols)),
            fixed((span, HEAD_DIM)),
            fixed((span, HEAD_DIM)),
        ],
        [
            pl.BlockSpec((span, 2 * HEAD_DIM), lambda s, at: (s, 0)),
            pl.BlockSpec((1, span, 2 * HEAD_DIM), lambda s, at: (s, 0, 0)),
            pl.BlockSpec((width, span), lambda s, at: (0, s)),
            fixed((8, width)),
            fixed((tokens, width)),
            pl.BlockSpec((span, cols), lambda s, at: (s, 0)),
            pl.BlockSpec((span, 128), lambda s, at: (s, 0)),
        ],
        [
            shape((tokens, 2 * HEAD_DIM), BF),
            shape((2, span, 2 * HEAD_DIM), BF),
            shape((width, tokens), BF),
            shape((8, width), F32),
            shape((tokens, width), BF),
            shape((tokens, cols), BF),
            shape((tokens, 128), F32),
        ],
        [pltpu.VMEM((8, width), F32), pltpu.SemaphoreType.DMA((6,))],
        12,
        "norm_qkv_rope",
        (2.5, 10),
    )


def stacked(v):
    return jnp.concatenate([v[:, :HEAD_DIM], v[:, HEAD_DIM:]], axis=0)


def allowed_mask(low_ref, high_ref, length):
    low, high = low_ref[0], high_ref[...]
    places = lax.broadcasted_iota(jnp.int32, (length, low.shape[1]), 0)
    mask = (places >= low) & (places <= high)
    return jnp.concatenate([mask, mask], axis=1)


def attend_kernel(q_ref, kv_ref, low_ref, high_ref, out_ref, lse_ref, peak_ref):
    length = kv_ref.shape[1]
    span = q_ref.shape[0]
    queries = stacked(q_ref[...])
    keys, values = kv_ref[0, :, :HEAD_DIM], kv_ref[0, :, HEAD_DIM:]
    raw = dot(keys, queries, NT)
    scores = jnp.where(allowed_mask(low_ref, high_ref, length), raw * HEAD_DIM**-0.5, -1e30)
    largest = jnp.max(scores, axis=0, keepdims=True)
    weights = jnp.exp(scores - largest)
    total = jnp.sum(weights, axis=0, keepdims=True)
    probs = (weights * (1.0 / total)).astype(BF)
    attended = dot(values, probs, TN).T.astype(BF)
    out_ref[...] = jnp.concatenate([attended[:span], attended[span:]], axis=1)
    lse_ref[0] = largest + jnp.log(total)
    tops = [jnp.max(largest[:, h * span : (h + 1) * span], axis=1, keepdims=True) for h in (0, 1)]
    peak_ref[0] = jnp.concatenate([jnp.broadcast_to(t, (4, 128)) for t in tops], axis=0)


def attend_call(queries, kv, low, high):
    tokens = queries.shape[0]
    span, length, both = tokens // 2, kv.shape[1], 2 * HEAD_DIM
    return pl.pallas_call(
        attend_kernel,
        grid=(2,),
        in_specs=[
            pl.BlockSpec((span, both), lambda s: (s, 0)),
            pl.BlockSpec((1, length, both), lambda s: (s, 0, 0)),
            pl.BlockSpec((1, 1, span), lambda s: (s, 0, 0)),
            pl.BlockSpec((1, span), lambda s: (0, 0)),
        ],
        out_specs=[
            pl.BlockSpec((span, both), lambda s: (s, 0)),
            pl.BlockSpec((1, 1, 2 * span), lambda s: (s, 0, 0)),
            pl.BlockSpec((1, 8, 128), lambda s: (s, 0, 0)),
        ],
        out_shape=[
            shape((tokens, both), BF),
            shape((2, 1, 2 * span), F32),
            shape((2, 8, 128), F32),
        ],
        compiler_params=vmem(8),
        cost_estimate=cost(2.5, 4),
        name="attend",
    )(queries, kv, low, high)


def attend_back_kernel(
    q_ref, kv_ref, low_ref, high_ref, lse_ref, up_ref, cos_ref, sin_ref, dq_ref, dkv_ref
):
    length = kv_ref.shape[1]
    span = q_ref.shape[0]
    queries, upstream = stacked(q_ref[...]), stacked(up_ref[...])
    keys, values = kv_ref[0, :, :HEAD_DIM], kv_ref[0, :, HEAD_DIM:]
    raw = dot(keys, queries, NT)
    factor = HEAD_DIM**-0.5
    probs = jnp.where(
        allowed_mask(low_ref, high_ref, length), jnp.exp(raw * factor - lse_ref[0]), 0.0
    )
    dprobs = dot(values, upstream, NT)
    rowdot = jnp.sum(probs * dprobs, axis=0, keepdims=True)
    dscores = (probs * (dprobs - rowdot) * factor).astype(BF)
    dkey = dot(dscores, queries, NN)
    dvalue = dot(probs.astype(BF), upstream, NN)
    dkv_ref[0] = jnp.concatenate([dkey, dvalue], axis=1).astype(BF)
    dquery = dot(keys, dscores, TN).T
    cosine, sine = cos_ref[...], sin_ref[...]
    heads = []
    for h in (0, 1):
        d = dquery[h * span : (h + 1) * span]
        heads.append((d * cosine - roll_half(d) * sine).astype(BF))
    dq_ref[...] = jnp.concatenate(heads, axis=1)


def attend_back_call(queries, kv, low, high, lse, upstream, cosine, sine):
    tokens = queries.shape[0]
    span, length, both = tokens // 2, kv.shape[1], 2 * HEAD_DIM
    table = pl.BlockSpec((span, HEAD_DIM), lambda s: (0, 0))
    return pl.pallas_call(
        attend_back_kernel,
        grid=(2,),
        in_specs=[
            pl.BlockSpec((span, both), lambda s: (s, 0)),
            pl.BlockSpec((1, length, both), lambda s: (s, 0, 0)),
            pl.BlockSpec((1, 1, span), lambda s: (s, 0, 0)),
            pl.BlockSpec((1, span), lambda s: (0, 0)),
            pl.BlockSpec((1, 1, 2 * span), lambda s: (s, 0, 0)),
            pl.BlockSpec((span, both), lambda s: (s, 0)),
            table,
            table,
        ],
        out_specs=[
            pl.BlockSpec((span, both), lambda s: (s, 0)),
            pl.BlockSpec((1, length, both), lambda s: (s, 0, 0)),
        ],
        out_shape=[shape((tokens, both), BF), shape((2, length, both), BF)],
        compiler_params=vmem(10),
        cost_estimate=cost(4.5, 4),
        name="attend_back",
    )(queries, kv, low, high, lse, upstream, cosine, sine)


def ffn_kernel(at_ref, *refs):
    parts, refs = refs[:8], refs[8:]
    cot_hbm, cot_t_hbm, gain_hbm, wg_ref, wu_ref, wd_ref = refs[:6]
    act_ref, grad_ref, mid_ref, stat_ref = refs[6:10]
    normed_ref, flipped_ref, cot_ref, cot_t_ref, gain_ref, sems = refs[10:]
    step = pl.program_id(0)

    @pl.when(step == 0)
    def _():
        copies = [(gain_hbm, gain_ref), *assembled(at_ref, parts, mid_ref)]
        copies = bring(copies + [(cot_hbm, cot_ref), (cot_t_hbm, cot_t_ref)], sems)
        done(copies[:-2])

        @pl.loop(0, mid_ref.shape[0] // 128)
        def _(i):
            rows = pl.ds(pl.multiple_of(i * 128, 128), 128)
            mid = mid_ref[rows].astype(F32)
            scale = lax.rsqrt(jnp.mean(mid * mid, axis=-1, keepdims=True) + EPS)
            normed = (mid * scale * gain_ref[1:2]).astype(BF)
            normed_ref[rows] = normed
            flipped_ref[:, rows] = normed.T
            stat_ref[0, rows] = jnp.zeros((128, 128), F32)
            stat_ref[1, rows] = jnp.broadcast_to(scale, (128, 128))

        done(copies[-2:])

    normed = normed_ref[...]
    gate = dot(normed, wg_ref[...], NN)
    upper = dot(normed, wu_ref[...], NN)
    dhidden = dot(cot_ref[...], wd_ref[...], NN)
    sigmoid = 1.0 / (1.0 + jnp.exp(-gate))
    silu = gate * sigmoid
    slope = sigmoid * (1.0 + gate * (1.0 - sigmoid))
    dgate = (dhidden * upper * slope).astype(BF)
    dupper = (dhidden * silu).astype(BF)
    hidden = (silu * upper).astype(BF)
    act_ref[0] = dgate
    act_ref[1] = dupper
    act_ref[2] = hidden
    inner = jnp.sum(dgate.astype(F32) * gate + dupper.astype(F32) * upper, axis=-1, keepdims=True)
    stat_ref[0] += jnp.broadcast_to(inner, stat_ref.shape[1:])
    flipped = flipped_ref[...]
    for i, (left, right) in enumerate(((flipped, dgate), (flipped, dupper), (cot_t_ref[...], hidden))):
        grad = dot(left, right, NN).astype(BF)
        grad_ref[:, i] = grad.reshape(16, grad.shape[0] // 16, grad.shape[1])


def ffn_call(at, mid_parts, cot, cot_flipped, gains, w):
    tokens, width = cot.shape
    cols = w.shape[1] // 3
    block = 512
    steps = cols // block

    def columns(i):
        return pl.BlockSpec((width, block), lambda j, at: (0, i * steps + j))

    return call(
        ffn_kernel,
        at,
        steps,
        (*mid_parts, cot, cot_flipped, gains, w, w, w),
        far_off(11) + [columns(0), columns(1), columns(2)],
        [
            pl.BlockSpec((3, tokens, block), lambda j, at: (0, 0, j)),
            pl.BlockSpec((16, 3, width // 16, block), lambda j, at: (0, 0, 0, j)),
            fixed((tokens, width)),
            fixed((2, tokens, 128)),
        ],
        [
            shape((3, tokens, cols), BF),
            shape((16, 3, width // 16, cols), BF),
            shape((tokens, width), BF),
            shape((2, tokens, 128), F32),
        ],
        [
            pltpu.VMEM((tokens, width), BF),
            pltpu.VMEM((width, tokens), BF),
            pltpu.VMEM((tokens, width), BF),
            pltpu.VMEM((width, tokens), BF),
            pltpu.VMEM((8, width), F32),
            pltpu.SemaphoreType.DMA((11,)),
        ],
        60,
        "ffn",
        (16, 40),
    )


def norm_back(v, base, gain, stat):
    inner, scale = stat[0, :, 0:1], stat[1, :, 0:1]
    factor = scale * scale * inner / (4 * v.shape[1])
    return scale * (gain * v) - base.astype(F32) * factor


def send_order(v, step, keep_ref, give_ref):
    v = v.astype(BF)
    count = v.shape[0] // 2

    @pl.when(step == 0)
    def _():
        keep_ref[: 2 * count] = v

    @pl.when(step == 1)
    def _():
        give_ref[:count] = v[count:]
        give_ref[count : 2 * count] = v[:count]

    @pl.when(step >= 2)
    def _():
        at = pl.ds(pl.multiple_of(step * count, count), count)
        keep_ref[at] = v[:count]
        give_ref[at] = v[count:]


def back_kernel(terms, norm, at_ref, *refs):
    a_refs, w_refs, refs = refs[:terms], refs[terms : 2 * terms], refs[2 * terms :]
    v = sum(dot(a[0], w[...], NT) for a, w in zip(a_refs, w_refs))
    if norm is not None:
        base_ref, gain_ref, stat_ref, *refs = refs
        v = norm_back(v, base_ref[...], gain_ref[norm : norm + 1], stat_ref)
    if len(refs) == 4:
        block, beside, refs = v.shape[1], refs[:2], refs[2:]

        @pl.when(pl.program_id(0) == 0)
        def _():
            refs[0][:, block:] = beside[0][...]
            refs[1][:, block:] = beside[1][...]

        refs = [r.at[:, pl.ds(0, block)] for r in refs]
    send_order(v, pl.program_id(0), *refs)


def back_call(at, pairs, norm, extra, name, mib=12, beside=()):
    tokens, width = pairs[0][0].shape[1], pairs[0][2].shape[0]
    block = width // 4
    args, specs = [], []
    for a, i, _, _ in pairs:
        args.append(a)
        specs.append(pl.BlockSpec((1, tokens, a.shape[2]), lambda s, at, i=i: (i, 0, 0)))
    for a, _, w, j in pairs:
        args.append(w)
        specs.append(pl.BlockSpec((block, a.shape[2]), lambda s, at, j=j: (at[4 + s], j)))
    if norm is not None:
        args += extra
        specs += [
            pl.BlockSpec((tokens, block), lambda s, at: (0, at[4 + s])),
            pl.BlockSpec((8, block), lambda s, at: (0, at[4 + s])),
            fixed((2, tokens, 128)),
        ]
    args += beside
    specs += [fixed((2 * tokens, block)) for _ in beside]
    moved = (2 * tokens, 2 * block if beside else block)

    def kernel(*refs):
        back_kernel(len(pairs), norm, *refs)

    return call(
        kernel,
        at,
        4,
        args,
        specs,
        [fixed(moved)] * 2,
        [shape(moved, BF)] * 2,
        [],
        mib,
        name,
        (sum(1.2e-9 * 2 * tokens * width * a.shape[2] for a, *_ in pairs) + 1, 8),
    )


def proj_kernel(at_ref, *refs):
    parts, (w_ref, datt_ref, up_ref, sems) = refs[:8], refs[8:]
    done(bring(assembled(at_ref, parts, up_ref), sems))
    datt_ref[...] = dot(up_ref[...], w_ref[...], NN).astype(BF)


def proj_call(at, parts, w_proj, cols):
    tokens, width = 2 * parts[0].shape[0], w_proj.shape[0]
    return call(
        proj_kernel,
        at,
        1,
        (*parts, w_proj),
        far_off(8) + [fixed((width, cols))],
        [fixed((tokens, cols)), fixed((tokens, width))],
        [shape((tokens, cols), BF), shape((tokens, width), BF)],
        [pltpu.SemaphoreType.DMA((8,))],
        60,
        "proj_back",
        (1.5, 6),
    )


def proj_grad_kernel(up_ref, att_ref, grad_ref):
    grad_ref[...] = dot(att_ref[...], up_ref[...], TN).T.astype(BF)


def proj_grad_call(up, attended):
    return pl.pallas_call(
        proj_grad_kernel,
        out_shape=shape((up.shape[1], attended.shape[1]), BF),
        compiler_params=vmem(24),
        cost_estimate=cost(2, 4),
        name="proj_grad",
    )(up, attended)


def dkv_kernel(
    dq_ref, dkv_ref, near_ref, far_ref, raw_ref, scale_ref, cos_ref, sin_ref, nt_ref, proj_ref,
    d_ref, grad_ref, stat_ref,
):
    span = dkv_ref.shape[1]
    both = 2 * HEAD_DIM
    cosine, sine = cos_ref[...], sin_ref[...]
    d_ref[0, :, :both] = dq_ref[...]
    for s in (0, 1):
        dkv = sum(r[s].astype(F32) for r in (dkv_ref, near_ref, far_ref))
        dk = dkv[:, :HEAD_DIM]
        at = pl.ds(s * span, span)
        d_ref[0, at, both : 3 * HEAD_DIM] = (dk * cosine - roll_half(dk) * sine).astype(BF)
        d_ref[0, at, 3 * HEAD_DIM :] = dkv[:, HEAD_DIM:].astype(BF)
    d = d_ref[0]
    inner = jnp.sum(d.astype(F32) * raw_ref[...].astype(F32), axis=-1, keepdims=True)
    stat_ref[0] = jnp.broadcast_to(inner, stat_ref.shape[1:])
    stat_ref[1] = scale_ref[...]
    grad_ref[:, :both] = proj_ref[...]
    grad_ref[:, both:] = dot(nt_ref[...], d, NN).astype(BF)


def dkv_call(dq, dkv, near, far, raw, scale, cosine, sine, nt, proj_grad):
    tokens, width = dq.shape[0], nt.shape[0]
    both = 2 * HEAD_DIM
    return pl.pallas_call(
        dkv_kernel,
        out_shape=[
            shape((1, tokens, 2 * both), BF),
            shape((width, 3 * both), BF),
            shape((2, tokens, 128), F32),
        ],
        compiler_params=vmem(8),
        cost_estimate=cost(2, 8),
        name="dqkv",
    )(dq, dkv, near, far, raw, scale, cosine, sine, nt, proj_grad)


def local(
    activations,
    segment_ids,
    attn_gain,
    qkv_weight,
    proj_weight,
    ffn_gain,
    gate_weight,
    up_weight,
    down_weight,
    cotangent,
    clip_limit,
):
    core = lax.axis_index("c")
    at_x = lax.axis_index("x")
    at_y = lax.axis_index("y")
    at_z = lax.axis_index("z")
    _, span, width = activations.shape
    head_dim = HEAD_DIM
    rows_held = qkv_weight.shape[0]
    block = 2 * rows_held

    side = 1 - 2 * core
    at = [at_x, at_x - side, at_x + side, at_x + 2]
    at = jnp.stack(at + [at[2], at[1], at[3], at[0]]).astype(jnp.int32) % 4

    gains = jnp.concatenate(
        [attn_gain[:, None], ffn_gain[:, None], jnp.zeros((rows_held, 126), BF)], axis=1
    )

    def halves(parts, extra):
        own = jnp.concatenate([column_half(w, core) for w in parts] + extra, axis=1)
        away = jnp.concatenate([column_half(w, 1 - core) for w in parts] + extra, axis=1)
        return own, away

    def both_rows(own, other):
        return by_core(core, own, other).reshape(block, -1)

    rows_mine = swap_blocks(activations[0], 2, 4)
    cot_mine = swap_blocks(cotangent[0], 2, 4)
    own_rows = jnp.concatenate([rows_mine, cot_mine], axis=1)
    attn_own, attn_away = halves((qkv_weight, proj_weight.T), [gains])
    ffn_own, ffn_away = halves((gate_weight, up_weight, down_weight.T), [])
    attn_other, rows_other, ids_other = wave(swap(attn_away), swap(own_rows), swap(segment_ids))
    attn_shard = both_rows(attn_own, attn_other)
    a0, b0 = attn_shard[None, :, : 4 * head_dim], attn_shard[None, :, 4 * head_dim :]
    pair = jnp.concatenate([own_rows, rows_other], axis=0)

    *got, row_near, ffn_other = wave(
        *direct(a0, "y"), *direct(b0, "z"), along_x(pair), swap(ffn_away)
    )
    a1 = place(dict(zip((0, -1, 1, 2), (a0, *got[:3]))), at_y, 0)[:, None]
    b1 = place(dict(zip((0, -1, 1, 2), (b0, *got[3:]))), at_z, 0)[None]
    *got, row_far, row_near_other = wave(
        *near_two(a1, "z"), *near_two(b1, "y"), along_x(row_near[:span]), swap(row_near)
    )
    a_near, b_near = got[:2], got[2:]
    row_far_other = swap(row_far)
    ffn_shard = both_rows(ffn_own, after(ffn_other, a_near[0]))
    w_ffn = lax.all_gather(ffn_shard, ("y", "z"), axis=0, tiled=True)
    a_far_0, a_far_1, b_far_0, b_far_1, row_far_other = wave(
        *far_two(*a_near, "z", 2), *far_two(*b_near, "y", 2), row_far_other
    )

    def in_rows(v):
        return v.reshape(16 * block, -1)

    w_qkv = in_rows(placed(a1, a_near, (a_far_0, a_far_1), at_z, 1, 2))
    w_proj = in_rows(placed(b1, b_near, (b_far_0, b_far_1), at_y, 0, 2))
    row_parts = (pair, row_near, row_near_other, row_far, row_far_other)

    half = head_dim // 2
    freqs = 1.0 / THETA ** (jnp.arange(half, dtype=F32) * 2.0 / head_dim)
    places = at_z * span + jnp.arange(span)
    angles = places.astype(F32)[:, None] * freqs[None, :]
    cosine = jnp.cos(jnp.concatenate([angles, angles], axis=1))
    sine = jnp.sin(angles)
    sine = jnp.concatenate([-sine, sine], axis=1)
    ids = jnp.concatenate([segment_ids, ids_other], axis=0)
    query_ids = lax.dynamic_slice_in_dim(ids, at_z * span, span, 1)
    low = jnp.sum(ids[:, :, None] < query_ids[:, None, :], axis=1, dtype=jnp.int32)[:, None, :]
    high = places.astype(jnp.int32)[None, :]

    queries, kv_mine, normed_one_t, gain_rows, rows, raw, scale_one = qkv_call(
        at, row_parts, w_proj, w_qkv, cosine, sine
    )
    kv_near = wave(*near_two(kv_mine, "z"))
    cot, cot_flipped = cot_call(at, (after(pair, kv_near[0]), *row_parts[1:]))
    *kv_far, cot, cot_flipped = wave(*far_two(*kv_near, "z", 1), cot, cot_flipped)
    kv = placed(kv_mine, kv_near, kv_far, at_z, 1, 1)
    attended, lse, peak = attend_call(queries, kv, low, high)
    peak = jnp.max(peak, axis=0)
    keep, give = back_call(at, [(attended[None], 0, w_proj, 0)], None, [], "branch")

    (got,) = wave(swap(give))
    far, near_other, near, mine = sums(keep, got)
    near_other = along_x(near_other)
    far, other_peak = wave(along_x(far), shift(peak, "y", 1))
    peak = jnp.maximum(peak, other_peak)
    near, rest, other_peak = wave(near_sum(near, far), swap(near_other), shift(peak, "y", 2))
    peak = jnp.maximum(peak, other_peak)
    mid_mine = rows_mine.astype(F32) + all_sums(mine, near, rest)
    own = mid_mine.astype(BF)
    other = swap(own)
    near_other = along_x(other)
    near, other_peak = wave(along_x(own), shift(peak, "z", 1))
    peak = jnp.maximum(peak, other_peak)
    far, near_other, near_swap, other_peak = wave(
        along_x(near), near_other, swap(near), shift(peak, "z", 2)
    )
    peak = jnp.maximum(peak, other_peak)
    peak = jnp.stack([peak[0, 0], peak[4, 0]])
    far_swap, near_other_swap, other_peak = wave(swap(far), swap(near_other), swap(peak))
    peaks = by_core(core, peak, other_peak).reshape(-1)
    mid_parts = (own, other, near, near_other, near_other_swap, near_swap, far, far_swap)

    act, ffn_grads, mid, stat = ffn_call(at, mid_parts, cot, cot_flipped, gain_rows, w_ffn)
    ffn_sums = lax.psum_scatter(ffn_grads, ("y", "z"), scatter_dimension=0, tiled=True)
    keep, give = back_call(
        at, [(act, 0, w_ffn, 0), (act, 1, w_ffn, 1)], 1, [mid, gain_rows, stat], "ffn_back", 60
    )

    (got,) = wave(swap(give))
    far, near_other, near, mine = sums(keep, got)
    near_other = along_x(near_other)
    keep_out, give_out = back_call(
        at, [(after(act, far), 2, w_ffn, 2)], None, [], "ffn_out", 60
    )
    far, keep_out, give_out = wave(along_x(far), keep_out, give_out)
    near, rest = wave(near_sum(near, far), swap(near_other))
    dmid = cot_mine.astype(F32) + all_sums(mine, near, rest)
    own = dmid.astype(BF)
    other = swap(own)
    near_other = along_x(other)
    (near,) = wave(along_x(own))
    far, near_other, near_swap = wave(along_x(near), near_other, swap(near))
    far_swap, near_other_swap = wave(swap(far), swap(near_other))
    dmid_parts = (own, other, near, near_other, near_other_swap, near_swap, far, far_swap)
    dattended, up = proj_call(at, dmid_parts, w_proj, attended.shape[1])
    dq, dkv = attend_back_call(queries, kv, low, high, lse, dattended, cosine, sine)

    far_0, far_1 = wave(*reduce_far(dkv, "z", at_z, 1, 1))
    proj_grad = proj_grad_call(after(up, far_0), attended)
    near_0, near_1, proj_grad = wave(*reduce_near(dkv, (far_0, far_1), "z", at_z, 1, 1), proj_grad)
    dprojected, attn_grads, stat = dkv_call(
        dq, ring_block(dkv, at_z, 0, 1), near_0, near_1, raw, scale_one, cosine, sine,
        normed_one_t, proj_grad,
    )
    attn_sums = trade(attn_grads.reshape(16, block, -1), ("y", "z"))
    keep, give = back_call(
        at, [(dprojected, 0, w_qkv, 0)], 0, [rows, gain_rows, stat], "qkv_back", 12,
        (keep_out, give_out),
    )
    got, ffn_sums = wave(swap(give), ffn_sums)
    far, near_other, near, mine = sums(keep, got)
    near_other = along_x(near_other)

    def rows_of(sums, which):
        both = sums.astype(BF).reshape(-1, 2, rows_held, sums.shape[-1])
        return lax.dynamic_index_in_dim(both, which, 1, keepdims=False)

    def whole(own, other):
        return jnp.concatenate(list(by_core(core, own, other)), axis=1).astype(F32)

    far, ffn_other, attn_sums = wave(
        along_x(far), swap(rows_of(ffn_sums, 1 - core)), attn_sums
    )
    own = rows_of(ffn_sums, core)
    gate_part, up_part, down_part = (whole(own[i], ffn_other[i]) for i in range(3))
    gain_two_sum = jnp.sum(gate_weight.astype(F32) * gate_part, axis=1) + jnp.sum(
        up_weight.astype(F32) * up_part, axis=1
    )
    near, rest = wave(near_sum(near, far), swap(near_other))
    attn_sums = added(attn_sums)
    other = swap(rows_of(attn_sums, 1 - core))[0]
    in_sums = all_sums(mine, near, rest)
    input_grad = swap_blocks(dmid + in_sums[:, :width], 4, 2)[None]
    output = swap_blocks((mid_mine + in_sums[:, width:]).astype(BF), 4, 2)[None]
    both = 2 * head_dim
    own = rows_of(attn_sums, core)[0]
    proj_part = whole(own[:, :both], other[:, :both])
    qkv_part = whole(own[:, both:], other[:, both:])

    gain_sums = jnp.stack([jnp.sum(qkv_weight.astype(F32) * qkv_part, axis=1), gain_two_sum])
    gain_sums = sum(direct(gain_sums, "x"), gain_sums)
    gain_one_grad = gain_sums[0] / attn_gain.astype(F32)
    gain_two_grad = gain_sums[1] / ffn_gain.astype(F32)

    bound = clip_limit[0]
    groups = 2
    factors = jnp.sqrt(bound / jnp.maximum(peaks, bound)).reshape(groups, 2)
    column_scale = jnp.concatenate(
        [factors, jnp.min(factors, axis=1, keepdims=True), jnp.ones((groups, 1), F32)], axis=1
    )
    clipped = (
        qkv_weight.astype(F32).reshape(rows_held, groups, 4, head_dim)
        * column_scale[None, :, :, None]
    ).reshape(rows_held, -1)
    return (
        output,
        input_grad,
        qkv_part,
        proj_part.T,
        gain_one_grad,
        gate_part,
        up_part,
        down_part.T,
        gain_two_grad,
        peaks,
        clipped,
    )


def solution(mesh):
    fine = Mesh(mesh.devices.reshape(4, 2, 4, 4), ("y", "c", "z", "x"))
    rows = ("y", "c", "z")
    act = P(("y", "c"), "z", "x")
    weight = P(rows, "x")
    flipped = P("x", rows)
    return jax.shard_map(
        local,
        mesh=fine,
        in_specs=(
            act, P(("y", "c"), None), P(rows), weight, flipped, P(rows),
            weight, weight, flipped, act, P(),
        ),
        out_specs=(
            act, act, weight, flipped, P(rows), weight, weight, flipped, P(rows), P("x"), weight,
        ),
        check_vma=False,
    )
```

```python
import jax
import jax.numpy as jnp
from jax import lax
from jax.experimental import pallas as pl
from jax.experimental.pallas import tpu as pltpu
from jax.sharding import Mesh
from jax.sharding import PartitionSpec as P

HEAD_DIM = 128
EPS = 1e-05
THETA = 1000000.0
BF = jnp.bfloat16
F32 = jnp.float32
MIB = 1024 * 1024

NN = (((1,), (0,)), ((), ()))
NT = (((1,), (1,)), ((), ()))
TN = (((0,), (0,)), ((), ()))


def dot(a, b, dims):
    return lax.dot_general(a, b, dims, preferred_element_type=F32)


def shape(dims, kind):
    return jax.ShapeDtypeStruct(dims, kind)


def vmem(mib):
    return pltpu.CompilerParams(vmem_limit_bytes=mib * MIB)


def cost(gflop, mib):
    return pl.CostEstimate(
        flops=int(gflop * 1e9), bytes_accessed=int(mib * MIB), transcendentals=0
    )


def shift(v, axis, k):
    n = lax.axis_size(axis)
    return lax.ppermute(v, axis, [(i, (i + k) % n) for i in range(n)])


def swap(v):
    return shift(v, "c", 1)


def column_half(w, which):
    half = w.shape[1] // 2
    return lax.dynamic_slice_in_dim(w, which * half, half, 1)


def by_core(core, own, other):
    return jnp.where(core == 0, jnp.stack([own, other]), jnp.stack([other, own]))


def place(pieces, at, dim):
    own = pieces[0]
    width = own.shape[dim]
    dims = own.shape[:dim] + (4 * width,) + own.shape[dim + 1 :]
    out = jnp.zeros(dims, own.dtype)
    for k, piece in pieces.items():
        out = lax.dynamic_update_slice_in_dim(out, piece, ((at + k) % 4) * width, dim)
    return out


def wave(*arrays):
    return lax.optimization_barrier(arrays)


def after(v, *others):
    return lax.optimization_barrier((v, *others))[0]


def direct(own, axis):
    return shift(own, axis, 1), shift(own, axis, -1), shift(own, axis, 2)


def halves_of(v, cut):
    half = v.shape[cut] // 2
    return lax.slice_in_dim(v, 0, half, axis=cut), lax.slice_in_dim(v, half, 2 * half, axis=cut)


def near_two(own, axis):
    return shift(own, axis, 1), shift(own, axis, -1)


def far_two(before, behind, axis, cut):
    return shift(halves_of(before, cut)[0], axis, 1), shift(halves_of(behind, cut)[1], axis, -1)


def placed(own, near, far, at, dim, cut):
    return place({0: own, -1: near[0], 1: near[1], 2: jnp.concatenate(far, axis=cut)}, at, dim)


def ring_block(v, at, k, dim):
    width = v.shape[dim] // 4
    return lax.dynamic_slice_in_dim(v, ((at + k) % 4) * width, width, dim)


def reduce_far(v, axis, at, dim, cut):
    low, high = halves_of(ring_block(v, at, 2, dim), cut)
    return shift(low, axis, 1), shift(high, axis, -1)


def reduce_near(v, far, axis, at, dim, cut):
    zeros = jnp.zeros_like(far[0])
    up = ring_block(v, at, 1, dim).astype(F32) + jnp.concatenate([far[0], zeros], axis=cut)
    down = ring_block(v, at, -1, dim).astype(F32) + jnp.concatenate([zeros, far[1]], axis=cut)
    return shift(up.astype(BF), axis, 1), shift(down.astype(BF), axis, -1)


def trade(v, axis):
    return lax.all_to_all(v, axis, split_axis=0, concat_axis=0, tiled=True)


def added(v):
    return jnp.sum(v.astype(F32), axis=0)


def total(v, at, dim, parts):
    return sum((p.astype(F32) for p in parts), ring_block(v, at, 0, dim).astype(F32))


def along_x(v):
    return lax.ppermute(
        v, ("c", "x"), [(4 * c + x, 4 * c + (x + 1 - 2 * c) % 4) for c in (0, 1) for x in range(4)]
    )


def sums_kernel(keep_ref, got_ref, far_ref, near_other_ref, near_ref, mine_ref):
    count = far_ref.shape[0]

    def section(k):
        at = pl.ds(k * count, count)
        return keep_ref[at].astype(F32) + got_ref[at].astype(F32)

    far_ref[...] = section(2).astype(BF)
    near_other_ref[...] = section(1).astype(BF)
    near_ref[...] = section(0)
    mine_ref[...] = section(3)


def sums(keep, got):
    rows, width = keep.shape
    part = (rows // 4, width)
    return pl.pallas_call(
        sums_kernel,
        out_shape=[shape(part, BF), shape(part, BF), shape(part, F32), shape(part, F32)],
        compiler_params=vmem(60),
        cost_estimate=cost(0, 6),
        name="sums",
    )(keep, got)


def near_sum(near, far):
    return along_x((near + far.astype(F32)).astype(BF))


def all_sums(mine, near, rest):
    return mine + near.astype(F32) + rest.astype(F32)


def swap_blocks(v, first, second):
    rows = v.shape[0]
    return v.reshape(rows, first, second, -1).swapaxes(1, 2).reshape(rows, -1)


def roll_half(v):
    return pltpu.roll(v, 64, 1)


def lanes(block):
    return pl.ds(pl.multiple_of(block * 512, 512), 512)


def bring(copies, sems, first=0):
    copies = [pltpu.make_async_copy(a, b, sems.at[first + i]) for i, (a, b) in enumerate(copies)]
    for c in copies:
        c.start()
    return copies


def done(copies):
    for c in copies:
        c.wait()


def assembled(at_ref, parts, out_ref):
    count = parts[0].shape[0]
    return [
        (parts[2 * k + i], out_ref.at[pl.ds(i * count, count), lanes(at_ref[k])])
        for k in range(4)
        for i in (0, 1)
    ]


def assembled_rows(at_ref, parts, column, out_ref):
    pair, near, other_near, far, other_far = (
        p.at[:, pl.ds(column * 512, 512)] for p in parts
    )
    count = far.shape[0]
    low, high = pl.ds(0, count), pl.ds(count, count)
    return [
        (pair, out_ref.at[:, lanes(at_ref[0])]),
        (near, out_ref.at[:, lanes(at_ref[1])]),
        (other_near.at[high], out_ref.at[low, lanes(at_ref[2])]),
        (other_near.at[low], out_ref.at[high, lanes(at_ref[2])]),
        (far, out_ref.at[low, lanes(at_ref[3])]),
        (other_far, out_ref.at[high, lanes(at_ref[3])]),
    ]


def far_off(count):
    return [pl.BlockSpec(memory_space=pltpu.HBM)] * count


def fixed(dims):
    return pl.BlockSpec(dims, lambda s, at: (0,) * len(dims))


def call(kernel, at, grid, args, in_specs, out_specs, out_shape, scratch, mib, name, work):
    return pl.pallas_call(
        kernel,
        grid_spec=pltpu.PrefetchScalarGridSpec(
            num_scalar_prefetch=1,
            grid=(grid,),
            in_specs=in_specs,
            out_specs=out_specs,
            scratch_shapes=scratch,
        ),
        out_shape=out_shape,
        compiler_params=vmem(mib),
        cost_estimate=cost(*work),
        name=name,
    )(at, *args)


def qkv_kernel(at_ref, *refs):
    parts, refs = refs[:5], refs[5:]
    gains_ref, w_ref, cos_ref, sin_ref = refs[:4]
    q_ref, kv_ref, nt_ref, row_ref, rows_ref, raw_ref, scale_ref, keep, sems = refs[4:]
    step = pl.program_id(0)
    span = q_ref.shape[0]

    @pl.when(step == 0)
    def _():
        copies = bring(assembled_rows(at_ref, parts, 0, rows_ref), sems)
        keep[...] = gains_ref[...].astype(F32).T[:8]
        row_ref[...] = keep[...]
        done(copies)

    rows = rows_ref[pl.ds(pl.multiple_of(step * span, span), span)].astype(F32)
    scale = lax.rsqrt(jnp.mean(rows * rows, axis=-1, keepdims=True) + EPS)
    normed = (rows * scale * keep[0:1]).astype(BF)
    nt_ref[...] = normed.T
    projected = dot(normed, w_ref[...], NN)
    raw_ref[...] = projected.astype(BF)
    scale_ref[...] = jnp.broadcast_to(scale, scale_ref.shape)
    cosine, sine = cos_ref[...], sin_ref[...]
    out = []
    for i in range(3):
        v = projected[:, i * HEAD_DIM : (i + 1) * HEAD_DIM]
        out.append((v * cosine + roll_half(v) * sine).astype(BF))
    q_ref[...] = jnp.concatenate(out[:2], axis=1)
    kv_ref[0] = jnp.concatenate([out[2], projected[:, 3 * HEAD_DIM :].astype(BF)], axis=1)


def cot_kernel(at_ref, *refs):
    parts, (out_ref, flipped_ref, sems) = refs[:5], refs[5:]
    done(bring(assembled_rows(at_ref, parts, 1, out_ref), sems))
    flipped_ref[...] = out_ref[...].T


def cot_call(at, parts):
    tokens, width = parts[0].shape[0], 4 * 512
    return call(
        cot_kernel,
        at,
        1,
        parts,
        far_off(5),
        [fixed((tokens, width)), fixed((width, tokens))],
        [shape((tokens, width), BF), shape((width, tokens), BF)],
        [pltpu.SemaphoreType.DMA((6,))],
        12,
        "cotangent_rows",
        (0.5, 8),
    )


def qkv_call(at, parts, gains, w_qkv, cosine, sine):
    tokens, (width, cols) = parts[0].shape[0], w_qkv.shape
    span = tokens // 2
    return call(
        qkv_kernel,
        at,
        2,
        (*parts, gains, w_qkv, cosine, sine),
        far_off(5)
        + [
            pl.BlockSpec((width, 128), lambda s, at: (0, 2)),
            fixed((width, cols)),
            fixed((span, HEAD_DIM)),
            fixed((span, HEAD_DIM)),
        ],
        [
            pl.BlockSpec((span, 2 * HEAD_DIM), lambda s, at: (s, 0)),
            pl.BlockSpec((1, span, 2 * HEAD_DIM), lambda s, at: (s, 0, 0)),
            pl.BlockSpec((width, span), lambda s, at: (0, s)),
            fixed((8, width)),
            fixed((tokens, width)),
            pl.BlockSpec((span, cols), lambda s, at: (s, 0)),
            pl.BlockSpec((span, 128), lambda s, at: (s, 0)),
        ],
        [
            shape((tokens, 2 * HEAD_DIM), BF),
            shape((2, span, 2 * HEAD_DIM), BF),
            shape((width, tokens), BF),
            shape((8, width), F32),
            shape((tokens, width), BF),
            shape((tokens, cols), BF),
            shape((tokens, 128), F32),
        ],
        [pltpu.VMEM((8, width), F32), pltpu.SemaphoreType.DMA((6,))],
        12,
        "norm_qkv_rope",
        (2.5, 10),
    )


def stacked(v):
    return jnp.concatenate([v[:, :HEAD_DIM], v[:, HEAD_DIM:]], axis=0)


def allowed_mask(low_ref, high_ref, length):
    low, high = low_ref[0], high_ref[...]
    places = lax.broadcasted_iota(jnp.int32, (length, low.shape[1]), 0)
    mask = (places >= low) & (places <= high)
    return jnp.concatenate([mask, mask], axis=1)


def attend_kernel(q_ref, kv_ref, low_ref, high_ref, out_ref, lse_ref, peak_ref):
    length = kv_ref.shape[1]
    span = q_ref.shape[0]
    queries = stacked(q_ref[...])
    keys, values = kv_ref[0, :, :HEAD_DIM], kv_ref[0, :, HEAD_DIM:]
    raw = dot(keys, queries, NT)
    scores = jnp.where(allowed_mask(low_ref, high_ref, length), raw * HEAD_DIM**-0.5, -1e30)
    largest = jnp.max(scores, axis=0, keepdims=True)
    weights = jnp.exp(scores - largest)
    total = jnp.sum(weights, axis=0, keepdims=True)
    probs = (weights * (1.0 / total)).astype(BF)
    attended = dot(values, probs, TN).T.astype(BF)
    out_ref[...] = jnp.concatenate([attended[:span], attended[span:]], axis=1)
    lse_ref[0] = largest + jnp.log(total)
    tops = [jnp.max(largest[:, h * span : (h + 1) * span], axis=1, keepdims=True) for h in (0, 1)]
    peak_ref[0] = jnp.concatenate([jnp.broadcast_to(t, (4, 128)) for t in tops], axis=0)


def attend_call(queries, kv, low, high):
    tokens = queries.shape[0]
    span, length, both = tokens // 2, kv.shape[1], 2 * HEAD_DIM
    return pl.pallas_call(
        attend_kernel,
        grid=(2,),
        in_specs=[
            pl.BlockSpec((span, both), lambda s: (s, 0)),
            pl.BlockSpec((1, length, both), lambda s: (s, 0, 0)),
            pl.BlockSpec((1, 1, span), lambda s: (s, 0, 0)),
            pl.BlockSpec((1, span), lambda s: (0, 0)),
        ],
        out_specs=[
            pl.BlockSpec((span, both), lambda s: (s, 0)),
            pl.BlockSpec((1, 1, 2 * span), lambda s: (s, 0, 0)),
            pl.BlockSpec((1, 8, 128), lambda s: (s, 0, 0)),
        ],
        out_shape=[
            shape((tokens, both), BF),
            shape((2, 1, 2 * span), F32),
            shape((2, 8, 128), F32),
        ],
        compiler_params=vmem(8),
        cost_estimate=cost(2.5, 4),
        name="attend",
    )(queries, kv, low, high)


def attend_back_kernel(
    q_ref, kv_ref, low_ref, high_ref, lse_ref, up_ref, cos_ref, sin_ref, dq_ref, dkv_ref
):
    length = kv_ref.shape[1]
    span = q_ref.shape[0]
    queries, upstream = stacked(q_ref[...]), stacked(up_ref[...])
    keys, values = kv_ref[0, :, :HEAD_DIM], kv_ref[0, :, HEAD_DIM:]
    raw = dot(keys, queries, NT)
    factor = HEAD_DIM**-0.5
    probs = jnp.where(
        allowed_mask(low_ref, high_ref, length), jnp.exp(raw * factor - lse_ref[0]), 0.0
    )
    dprobs = dot(values, upstream, NT)
    rowdot = jnp.sum(probs * dprobs, axis=0, keepdims=True)
    dscores = (probs * (dprobs - rowdot) * factor).astype(BF)
    dkey = dot(dscores, queries, NN)
    dvalue = dot(probs.astype(BF), upstream, NN)
    dkv_ref[0] = jnp.concatenate([dkey, dvalue], axis=1).astype(BF)
    dquery = dot(keys, dscores, TN).T
    cosine, sine = cos_ref[...], sin_ref[...]
    heads = []
    for h in (0, 1):
        d = dquery[h * span : (h + 1) * span]
        heads.append((d * cosine - roll_half(d) * sine).astype(BF))
    dq_ref[...] = jnp.concatenate(heads, axis=1)


def attend_back_call(queries, kv, low, high, lse, upstream, cosine, sine):
    tokens = queries.shape[0]
    span, length, both = tokens // 2, kv.shape[1], 2 * HEAD_DIM
    table = pl.BlockSpec((span, HEAD_DIM), lambda s: (0, 0))
    return pl.pallas_call(
        attend_back_kernel,
        grid=(2,),
        in_specs=[
            pl.BlockSpec((span, both), lambda s: (s, 0)),
            pl.BlockSpec((1, length, both), lambda s: (s, 0, 0)),
            pl.BlockSpec((1, 1, span), lambda s: (s, 0, 0)),
            pl.BlockSpec((1, span), lambda s: (0, 0)),
            pl.BlockSpec((1, 1, 2 * span), lambda s: (s, 0, 0)),
            pl.BlockSpec((span, both), lambda s: (s, 0)),
            table,
            table,
        ],
        out_specs=[
            pl.BlockSpec((span, both), lambda s: (s, 0)),
            pl.BlockSpec((1, length, both), lambda s: (s, 0, 0)),
        ],
        out_shape=[shape((tokens, both), BF), shape((2, length, both), BF)],
        compiler_params=vmem(10),
        cost_estimate=cost(4.5, 4),
        name="attend_back",
    )(queries, kv, low, high, lse, upstream, cosine, sine)


def ffn_kernel(at_ref, *refs):
    parts, refs = refs[:8], refs[8:]
    cot_hbm, cot_t_hbm, gain_hbm, wg_ref, wu_ref, wd_ref = refs[:6]
    act_ref, grad_ref, mid_ref, stat_ref = refs[6:10]
    normed_ref, flipped_ref, cot_ref, cot_t_ref, gain_ref, sems = refs[10:]
    step = pl.program_id(0)

    @pl.when(step == 0)
    def _():
        copies = [(gain_hbm, gain_ref), *assembled(at_ref, parts, mid_ref)]
        copies = bring(copies + [(cot_hbm, cot_ref), (cot_t_hbm, cot_t_ref)], sems)
        done(copies[:-2])

        @pl.loop(0, mid_ref.shape[0] // 128)
        def _(i):
            rows = pl.ds(pl.multiple_of(i * 128, 128), 128)
            mid = mid_ref[rows].astype(F32)
            scale = lax.rsqrt(jnp.mean(mid * mid, axis=-1, keepdims=True) + EPS)
            normed = (mid * scale * gain_ref[1:2]).astype(BF)
            normed_ref[rows] = normed
            flipped_ref[:, rows] = normed.T
            stat_ref[0, rows] = jnp.zeros((128, 128), F32)
            stat_ref[1, rows] = jnp.broadcast_to(scale, (128, 128))

        done(copies[-2:])

    normed = normed_ref[...]
    gate = dot(normed, wg_ref[...], NN)
    upper = dot(normed, wu_ref[...], NN)
    dhidden = dot(cot_ref[...], wd_ref[...], NN)
    sigmoid = 1.0 / (1.0 + jnp.exp(-gate))
    silu = gate * sigmoid
    slope = sigmoid * (1.0 + gate * (1.0 - sigmoid))
    dgate = (dhidden * upper * slope).astype(BF)
    dupper = (dhidden * silu).astype(BF)
    hidden = (silu * upper).astype(BF)
    act_ref[0] = dgate
    act_ref[1] = dupper
    act_ref[2] = hidden
    inner = jnp.sum(dgate.astype(F32) * gate + dupper.astype(F32) * upper, axis=-1, keepdims=True)
    stat_ref[0] += jnp.broadcast_to(inner, stat_ref.shape[1:])
    flipped = flipped_ref[...]
    for i, (left, right) in enumerate(((flipped, dgate), (flipped, dupper), (cot_t_ref[...], hidden))):
        grad = dot(left, right, NN).astype(BF)
        grad_ref[:, i] = grad.reshape(16, grad.shape[0] // 16, grad.shape[1])


def ffn_call(at, mid_parts, cot, cot_flipped, gains, w):
    tokens, width = cot.shape
    cols = w.shape[1] // 3
    block = 512
    steps = cols // block

    def columns(i):
        return pl.BlockSpec((width, block), lambda j, at: (0, i * steps + j))

    return call(
        ffn_kernel,
        at,
        steps,
        (*mid_parts, cot, cot_flipped, gains, w, w, w),
        far_off(11) + [columns(0), columns(1), columns(2)],
        [
            pl.BlockSpec((3, tokens, block), lambda j, at: (0, 0, j)),
            pl.BlockSpec((16, 3, width // 16, block), lambda j, at: (0, 0, 0, j)),
            fixed((tokens, width)),
            fixed((2, tokens, 128)),
        ],
        [
            shape((3, tokens, cols), BF),
            shape((16, 3, width // 16, cols), BF),
            shape((tokens, width), BF),
            shape((2, tokens, 128), F32),
        ],
        [
            pltpu.VMEM((tokens, width), BF),
            pltpu.VMEM((width, tokens), BF),
            pltpu.VMEM((tokens, width), BF),
            pltpu.VMEM((width, tokens), BF),
            pltpu.VMEM((8, width), F32),
            pltpu.SemaphoreType.DMA((11,)),
        ],
        60,
        "ffn",
        (16, 40),
    )


def norm_back(v, base, gain, stat):
    inner, scale = stat[0, :, 0:1], stat[1, :, 0:1]
    factor = scale * scale * inner / (4 * v.shape[1])
    return scale * (gain * v) - base.astype(F32) * factor


def send_order(v, step, keep_ref, give_ref):
    v = v.astype(BF)
    count = v.shape[0] // 2

    @pl.when(step == 0)
    def _():
        keep_ref[: 2 * count] = v

    @pl.when(step == 1)
    def _():
        give_ref[:count] = v[count:]
        give_ref[count : 2 * count] = v[:count]

    @pl.when(step >= 2)
    def _():
        at = pl.ds(pl.multiple_of(step * count, count), count)
        keep_ref[at] = v[:count]
        give_ref[at] = v[count:]


def back_kernel(terms, norm, at_ref, *refs):
    a_refs, w_refs, refs = refs[:terms], refs[terms : 2 * terms], refs[2 * terms :]
    v = sum(dot(a[0], w[...], NT) for a, w in zip(a_refs, w_refs))
    if norm is not None:
        base_ref, gain_ref, stat_ref, *refs = refs
        v = norm_back(v, base_ref[...], gain_ref[norm : norm + 1], stat_ref)
    if len(refs) == 4:
        block, beside, refs = v.shape[1], refs[:2], refs[2:]

        @pl.when(pl.program_id(0) == 0)
        def _():
            refs[0][:, block:] = beside[0][...]
            refs[1][:, block:] = beside[1][...]

        refs = [r.at[:, pl.ds(0, block)] for r in refs]
    send_order(v, pl.program_id(0), *refs)


def back_call(at, pairs, norm, extra, name, mib=12, beside=()):
    tokens, width = pairs[0][0].shape[1], pairs[0][2].shape[0]
    block = width // 4
    args, specs = [], []
    for a, i, _, _ in pairs:
        args.append(a)
        specs.append(pl.BlockSpec((1, tokens, a.shape[2]), lambda s, at, i=i: (i, 0, 0)))
    for a, _, w, j in pairs:
        args.append(w)
        specs.append(pl.BlockSpec((block, a.shape[2]), lambda s, at, j=j: (at[4 + s], j)))
    if norm is not None:
        args += extra
        specs += [
            pl.BlockSpec((tokens, block), lambda s, at: (0, at[4 + s])),
            pl.BlockSpec((8, block), lambda s, at: (0, at[4 + s])),
            fixed((2, tokens, 128)),
        ]
    args += beside
    specs += [fixed((2 * tokens, block)) for _ in beside]
    moved = (2 * tokens, 2 * block if beside else block)

    def kernel(*refs):
        back_kernel(len(pairs), norm, *refs)

    return call(
        kernel,
        at,
        4,
        args,
        specs,
        [fixed(moved)] * 2,
        [shape(moved, BF)] * 2,
        [],
        mib,
        name,
        (sum(1.2e-9 * 2 * tokens * width * a.shape[2] for a, *_ in pairs) + 1, 8),
    )


def proj_kernel(at_ref, *refs):
    parts, (w_ref, datt_ref, up_ref, sems) = refs[:8], refs[8:]
    done(bring(assembled(at_ref, parts, up_ref), sems))
    datt_ref[...] = dot(up_ref[...], w_ref[...], NN).astype(BF)


def proj_call(at, parts, w_proj, cols):
    tokens, width = 2 * parts[0].shape[0], w_proj.shape[0]
    return call(
        proj_kernel,
        at,
        1,
        (*parts, w_proj),
        far_off(8) + [fixed((width, cols))],
        [fixed((tokens, cols)), fixed((tokens, width))],
        [shape((tokens, cols), BF), shape((tokens, width), BF)],
        [pltpu.SemaphoreType.DMA((8,))],
        60,
        "proj_back",
        (1.5, 6),
    )


def proj_grad_kernel(up_ref, att_ref, grad_ref):
    grad_ref[...] = dot(att_ref[...], up_ref[...], TN).T.astype(BF)


def proj_grad_call(up, attended):
    return pl.pallas_call(
        proj_grad_kernel,
        out_shape=shape((up.shape[1], attended.shape[1]), BF),
        compiler_params=vmem(24),
        cost_estimate=cost(2, 4),
        name="proj_grad",
    )(up, attended)


def dkv_kernel(
    dq_ref, dkv_ref, near_ref, far_ref, raw_ref, scale_ref, cos_ref, sin_ref, nt_ref, proj_ref,
    d_ref, grad_ref, stat_ref,
):
    span = dkv_ref.shape[1]
    both = 2 * HEAD_DIM
    cosine, sine = cos_ref[...], sin_ref[...]
    d_ref[0, :, :both] = dq_ref[...]
    for s in (0, 1):
        dkv = sum(r[s].astype(F32) for r in (dkv_ref, near_ref, far_ref))
        dk = dkv[:, :HEAD_DIM]
        at = pl.ds(s * span, span)
        d_ref[0, at, both : 3 * HEAD_DIM] = (dk * cosine - roll_half(dk) * sine).astype(BF)
        d_ref[0, at, 3 * HEAD_DIM :] = dkv[:, HEAD_DIM:].astype(BF)
    d = d_ref[0]
    inner = jnp.sum(d.astype(F32) * raw_ref[...].astype(F32), axis=-1, keepdims=True)
    stat_ref[0] = jnp.broadcast_to(inner, stat_ref.shape[1:])
    stat_ref[1] = scale_ref[...]
    grad_ref[:, :both] = proj_ref[...]
    grad_ref[:, both:] = dot(nt_ref[...], d, NN).astype(BF)


def dkv_call(dq, dkv, near, far, raw, scale, cosine, sine, nt, proj_grad):
    tokens, width = dq.shape[0], nt.shape[0]
    both = 2 * HEAD_DIM
    return pl.pallas_call(
        dkv_kernel,
        out_shape=[
            shape((1, tokens, 2 * both), BF),
            shape((width, 3 * both), BF),
            shape((2, tokens, 128), F32),
        ],
        compiler_params=vmem(8),
        cost_estimate=cost(2, 8),
        name="dqkv",
    )(dq, dkv, near, far, raw, scale, cosine, sine, nt, proj_grad)


def local(
    activations,
    segment_ids,
    attn_gain,
    qkv_weight,
    proj_weight,
    ffn_gain,
    gate_weight,
    up_weight,
    down_weight,
    cotangent,
    clip_limit,
):
    core = lax.axis_index("c")
    at_x = lax.axis_index("x")
    at_y = lax.axis_index("y")
    at_z = lax.axis_index("z")
    _, span, width = activations.shape
    head_dim = HEAD_DIM
    rows_held = qkv_weight.shape[0]
    block = 2 * rows_held

    side = 1 - 2 * core
    at = [at_x, at_x - side, at_x + side, at_x + 2]
    at = jnp.stack(at + [at[2], at[1], at[3], at[0]]).astype(jnp.int32) % 4

    gains = jnp.concatenate(
        [attn_gain[:, None], ffn_gain[:, None], jnp.zeros((rows_held, 126), BF)], axis=1
    )

    def halves(parts, extra):
        own = jnp.concatenate([column_half(w, core) for w in parts] + extra, axis=1)
        away = jnp.concatenate([column_half(w, 1 - core) for w in parts] + extra, axis=1)
        return own, away

    def both_rows(own, other):
        return by_core(core, own, other).reshape(block, -1)

    rows_mine = swap_blocks(activations[0], 2, 4)
    cot_mine = swap_blocks(cotangent[0], 2, 4)
    own_rows = jnp.concatenate([rows_mine, cot_mine], axis=1)
    attn_own, attn_away = halves((qkv_weight, proj_weight.T), [gains])
    ffn_own, ffn_away = halves((gate_weight, up_weight, down_weight.T), [])
    attn_other, rows_other, ids_other = wave(swap(attn_away), swap(own_rows), swap(segment_ids))
    attn_shard = both_rows(attn_own, attn_other)
    a0, b0 = attn_shard[None, :, : 4 * head_dim], attn_shard[None, :, 4 * head_dim :]
    pair = jnp.concatenate([own_rows, rows_other], axis=0)

    *got, row_near, ffn_other = wave(
        *direct(a0, "y"), *direct(b0, "z"), along_x(pair), swap(ffn_away)
    )
    a1 = place(dict(zip((0, -1, 1, 2), (a0, *got[:3]))), at_y, 0)[:, None]
    b1 = place(dict(zip((0, -1, 1, 2), (b0, *got[3:]))), at_z, 0)[None]
    *got, row_far, row_near_other = wave(
        *near_two(a1, "z"), *near_two(b1, "y"), along_x(row_near[:span]), swap(row_near)
    )
    a_near, b_near = got[:2], got[2:]
    row_far_other = swap(row_far)
    ffn_shard = both_rows(ffn_own, after(ffn_other, a_near[0]))
    w_ffn = lax.all_gather(ffn_shard, ("y", "z"), axis=0, tiled=True)
    a_far_0, a_far_1, b_far_0, b_far_1, row_far_other = wave(
        *far_two(*a_near, "z", 2), *far_two(*b_near, "y", 2), row_far_other
    )

    def in_rows(v):
        return v.reshape(16 * block, -1)

    w_qkv = in_rows(placed(a1, a_near, (a_far_0, a_far_1), at_z, 1, 2))
    w_proj = in_rows(placed(b1, b_near, (b_far_0, b_far_1), at_y, 0, 2))
    row_parts = (pair, row_near, row_near_other, row_far, row_far_other)

    half = head_dim // 2
    freqs = 1.0 / THETA ** (jnp.arange(half, dtype=F32) * 2.0 / head_dim)
    places = at_z * span + jnp.arange(span)
    angles = places.astype(F32)[:, None] * freqs[None, :]
    cosine = jnp.cos(jnp.concatenate([angles, angles], axis=1))
    sine = jnp.sin(angles)
    sine = jnp.concatenate([-sine, sine], axis=1)
    ids = jnp.concatenate([segment_ids, ids_other], axis=0)
    query_ids = lax.dynamic_slice_in_dim(ids, at_z * span, span, 1)
    low = jnp.sum(ids[:, :, None] < query_ids[:, None, :], axis=1, dtype=jnp.int32)[:, None, :]
    high = places.astype(jnp.int32)[None, :]

    queries, kv_mine, normed_one_t, gain_rows, rows, raw, scale_one = qkv_call(
        at, row_parts, w_proj, w_qkv, cosine, sine
    )
    kv_near = wave(*near_two(kv_mine, "z"))
    cot, cot_flipped = cot_call(at, (after(pair, kv_near[0]), *row_parts[1:]))
    *kv_far, cot, cot_flipped = wave(*far_two(*kv_near, "z", 1), cot, cot_flipped)
    kv = placed(kv_mine, kv_near, kv_far, at_z, 1, 1)
    attended, lse, peak = attend_call(queries, kv, low, high)
    peak = jnp.max(peak, axis=0)
    keep, give = back_call(at, [(attended[None], 0, w_proj, 0)], None, [], "branch")

    (got,) = wave(swap(give))
    far, near_other, near, mine = sums(keep, got)
    near_other = along_x(near_other)
    far, other_peak = wave(along_x(far), shift(peak, "y", 1))
    peak = jnp.maximum(peak, other_peak)
    near, rest, other_peak = wave(near_sum(near, far), swap(near_other), shift(peak, "y", 2))
    peak = jnp.maximum(peak, other_peak)
    mid_mine = rows_mine.astype(F32) + all_sums(mine, near, rest)
    own = mid_mine.astype(BF)
    other = swap(own)
    near_other = along_x(other)
    near, other_peak = wave(along_x(own), shift(peak, "z", 1))
    peak = jnp.maximum(peak, other_peak)
    far, near_other, near_swap, other_peak = wave(
        along_x(near), near_other, swap(near), shift(peak, "z", 2)
    )
    peak = jnp.maximum(peak, other_peak)
    peak = jnp.stack([peak[0, 0], peak[4, 0]])
    far_swap, near_other_swap, other_peak = wave(swap(far), swap(near_other), swap(peak))
    peaks = by_core(core, peak, other_peak).reshape(-1)
    mid_parts = (own, other, near, near_other, near_other_swap, near_swap, far, far_swap)

    act, ffn_grads, mid, stat = ffn_call(at, mid_parts, cot, cot_flipped, gain_rows, w_ffn)
    ffn_sums = lax.psum_scatter(ffn_grads, ("y", "z"), scatter_dimension=0, tiled=True)
    keep, give = back_call(
        at, [(act, 0, w_ffn, 0), (act, 1, w_ffn, 1)], 1, [mid, gain_rows, stat], "ffn_back", 60
    )

    (got,) = wave(swap(give))
    far, near_other, near, mine = sums(keep, got)
    near_other = along_x(near_other)
    keep_out, give_out = back_call(
        at, [(after(act, far), 2, w_ffn, 2)], None, [], "ffn_out", 60
    )
    far, keep_out, give_out = wave(along_x(far), keep_out, give_out)
    near, rest = wave(near_sum(near, far), swap(near_other))
    dmid = cot_mine.astype(F32) + all_sums(mine, near, rest)
    own = dmid.astype(BF)
    other = swap(own)
    near_other = along_x(other)
    (near,) = wave(along_x(own))
    far, near_other, near_swap = wave(along_x(near), near_other, swap(near))
    far_swap, near_other_swap = wave(swap(far), swap(near_other))
    dmid_parts = (own, other, near, near_other, near_other_swap, near_swap, far, far_swap)
    dattended, up = proj_call(at, dmid_parts, w_proj, attended.shape[1])
    dq, dkv = attend_back_call(queries, kv, low, high, lse, dattended, cosine, sine)

    far_0, far_1 = wave(*reduce_far(dkv, "z", at_z, 1, 1))
    proj_grad = proj_grad_call(after(up, far_0), attended)
    near_0, near_1, proj_grad = wave(*reduce_near(dkv, (far_0, far_1), "z", at_z, 1, 1), proj_grad)
    dprojected, attn_grads, stat = dkv_call(
        dq, ring_block(dkv, at_z, 0, 1), near_0, near_1, raw, scale_one, cosine, sine,
        normed_one_t, proj_grad,
    )
    attn_sums = trade(attn_grads.reshape(16, block, -1), ("y", "z"))
    keep, give = back_call(
        at, [(dprojected, 0, w_qkv, 0)], 0, [rows, gain_rows, stat], "qkv_back", 60,
        (keep_out, give_out),
    )
    got, ffn_sums = wave(swap(give), ffn_sums)
    far, near_other, near, mine = sums(keep, got)
    near_other = along_x(near_other)

    def rows_of(sums, which):
        both = sums.astype(BF).reshape(-1, 2, rows_held, sums.shape[-1])
        return lax.dynamic_index_in_dim(both, which, 1, keepdims=False)

    def whole(own, other):
        return jnp.concatenate(list(by_core(core, own, other)), axis=1).astype(F32)

    far, ffn_other, attn_sums = wave(
        along_x(far), swap(rows_of(ffn_sums, 1 - core)), attn_sums
    )
    own = rows_of(ffn_sums, core)
    gate_part, up_part, down_part = (whole(own[i], ffn_other[i]) for i in range(3))
    gain_two_sum = jnp.sum(gate_weight.astype(F32) * gate_part, axis=1) + jnp.sum(
        up_weight.astype(F32) * up_part, axis=1
    )
    near, rest = wave(near_sum(near, far), swap(near_other))
    attn_sums = added(attn_sums)
    other = swap(rows_of(attn_sums, 1 - core))[0]
    in_sums = all_sums(mine, near, rest)
    input_grad = swap_blocks(dmid + in_sums[:, :width], 4, 2)[None]
    output = swap_blocks((mid_mine + in_sums[:, width:]).astype(BF), 4, 2)[None]
    both = 2 * head_dim
    own = rows_of(attn_sums, core)[0]
    proj_part = whole(own[:, :both], other[:, :both])
    qkv_part = whole(own[:, both:], other[:, both:])

    gain_sums = jnp.stack([jnp.sum(qkv_weight.astype(F32) * qkv_part, axis=1), gain_two_sum])
    gain_sums = sum(direct(gain_sums, "x"), gain_sums)
    gain_one_grad = gain_sums[0] / attn_gain.astype(F32)
    gain_two_grad = gain_sums[1] / ffn_gain.astype(F32)

    bound = clip_limit[0]
    groups = 2
    factors = jnp.sqrt(bound / jnp.maximum(peaks, bound)).reshape(groups, 2)
    column_scale = jnp.concatenate(
        [factors, jnp.min(factors, axis=1, keepdims=True), jnp.ones((groups, 1), F32)], axis=1
    )
    clipped = (
        qkv_weight.astype(F32).reshape(rows_held, groups, 4, head_dim)
        * column_scale[None, :, :, None]
    ).reshape(rows_held, -1)
    return (
        output,
        input_grad,
        qkv_part,
        proj_part.T,
        gain_one_grad,
        gate_part,
        up_part,
        down_part.T,
        gain_two_grad,
        peaks,
        clipped,
    )


def solution(mesh):
    fine = Mesh(mesh.devices.reshape(4, 2, 4, 4), ("y", "c", "z", "x"))
    rows = ("y", "c", "z")
    act = P(("y", "c"), "z", "x")
    weight = P(rows, "x")
    flipped = P("x", rows)
    return jax.shard_map(
        local,
        mesh=fine,
        in_specs=(
            act, P(("y", "c"), None), P(rows), weight, flipped, P(rows),
            weight, weight, flipped, act, P(),
        ),
        out_specs=(
            act, act, weight, flipped, P(rows), weight, weight, flipped, P(rows), P("x"), weight,
        ),
        check_vma=False,
    )
```
